128 devices in a mesh: de: 32 (over x, z, core), tp: 4 (over y).
Axes of the slice: x: 4, y: 4, z: 4, core: 2. Of those that a mesh axis runs over, the one named last changes fastest.
Arguments:
- raw_tiles: bfloat16 [4, 512, 512], P(None, ('de', 'tp')), may hold values from -6 to 6
- stem_weight: bfloat16 [48, 4, 3, 3], replicated, may hold values from -1 to 1
- embed_weight: bfloat16 [768, 1024], replicated, may hold values from -0.21875 to 0.21875
- norm_gain: float32 [1024], replicated, may hold values from 0.1 to 1.9
- router_weight: bfloat16 [1024, 32], replicated, may hold values from -0.1875 to 0.1875
- w_gate: bfloat16 [32, 1024, 4096], P('de', None, 'tp'), may hold values from -0.1875 to 0.1875
- w_up: bfloat16 [32, 1024, 4096], P('de', None, 'tp'), may hold values from -0.1875 to 0.1875
- w_down: bfloat16 [32, 4096, 1024], P('de', 'tp'), may hold values from -0.09375 to 0.09375
- routes: int32 [16384, 1], P(('de', 'tp')), may hold values from 0 to 31; in each aligned block of 128 rows (0 to 127, 128 to 255, ...) at most 8 rows name the same one
- cotangent: bfloat16 [16384, 1024], P(('de', 'tp')), may hold values from -6 to 6
Outputs:
- expert_mix: bfloat16 [16384, 1024], P(('de', 'tp'))
- grad_gate: float32 [32, 1024, 4096], P('de', None, 'tp')
- grad_up: float32 [32, 1024, 4096], P('de', None, 'tp')
- grad_down: float32 [32, 4096, 1024], P('de', 'tp')
- grad_router: float32 [1024, 32], replicated
- grad_gain: float32 [1024], replicated
- grad_embed: float32 [768, 1024], replicated
- grad_stem: float32 [48, 4, 3, 3], replicated
The draws below stay inside these ranges and needn't reach their ends.
Inputs may be any that keep to these rules, and one draw needn't show every extreme that they name: `routes`: within the tokens of one tile no expert is named more than 8 times, and in every draw some expert is named exactly 8 times in some tile.
All inputs are finite; a program needn't handle non-finite values.
Results may differ from the reference program's by a relative error of at most 0.0092.
Values may be sent and summed in bfloat16 or wider, within the bound.
No kernel may reach another device: no remote copies, remote signals or barrier semaphores. Data moves between devices by JAX's collectives and lax.ppermute only.
A program may use at most 128 MiB of HBM per device.

```python
import math
import jax
import jax.numpy as jnp
import numpy as np
from jax import lax

D = 1024
FF = 4096
STEM_CH = 48
PATCH = 4
TOP = 1
EXP_DEV = 1
TOK_DEV = 128
EXPERTS = 32
CAP = 8
TOKENS = 16384
ROWS = 512
COLS = 512
PATCH_DIM = 768
N_DE = 32
N_TP = 4


def shard_levels(stream_key, extent, cuts, low, largest):
    factor_of, own = 1.0, jax.random.fold_in(stream_key, 6)
    for position, blocks in cuts:
        heights = jnp.exp(jax.random.uniform(jax.random.fold_in(own, position), (blocks,), jnp.float32, low / len(cuts), largest / len(cuts)))
        factor_of = factor_of * jnp.repeat(heights, extent[position] // blocks).reshape([-1 if axis == position else 1 for axis in range(len(extent))])
    return factor_of


def assign_block(key, own, number, rows, count, top, reach, lean):
    order = jax.random.permutation(key, count)
    packed, common = load_shares(count, rows * top, reach, lean, True), load_shares(count, rows * top, reach, lean, False)
    places = jnp.arange(count)

    def named(tallies, turn):
        used = int((tallies > 0).sum())
        fixed = max(1, used // 4)
        moved = fixed + (places - fixed + turn * (used - fixed)) % max(1, count - fixed)
        return jnp.zeros((count,), jnp.int32).at[order[jnp.where(places < fixed, places, moved)]].set(jnp.asarray(tallies, jnp.int32))

    tallies = jnp.where(number % 4 == 0, named(packed, number // 4), named(common, number - number // 4 - 1))
    mixed = jax.random.permutation(jax.random.fold_in(own, 3), count)
    giver, sink = mixed[0:count // 2 * 2:2], mixed[1:count // 2 * 2:2]
    room = jnp.minimum(tallies[giver] - 1, reach - tallies[sink]) // 2
    room = jnp.where((giver == order[0]) | (sink == order[0]) | (tallies[sink] == 0), 0, jnp.maximum(room, 0))
    moved = jax.random.randint(jax.random.fold_in(own, 4), (count // 2,), 0, 1 << 20) % (room + 1)
    tallies = tallies.at[giver].add(-moved).at[sink].add(moved)
    items = jnp.searchsorted(jnp.cumsum(tallies), jnp.arange(rows * top), side="right").astype(jnp.int32)
    listing = items.reshape(top, rows).T
    listing = listing[jax.random.permutation(jax.random.fold_in(own, 1), rows)]
    turn = jax.random.randint(jax.random.fold_in(own, 2), (rows, 1), 0, top)
    return jnp.take_along_axis(listing, (jnp.arange(top)[None, :] + turn) % top, axis=1)


def load_shares(count, total, most, slope, full):
    weights = [(1 << 20) // math.isqrt(standing ** slope) + 1 for standing in range(1, count + 1)]
    largest = most if full else min(most, max(-(-total // count), total * weights[0] // sum(weights)))
    least = 1 if total - largest >= count - 1 else 0
    holding, spare = [largest] + [least] * (count - 1), total - largest - least * (count - 1)
    while spare > 0:
        candidates = [i for i in range(1, count) if holding[i] < largest] or [i for i in range(1, count) if holding[i] < most]
        mass, remaining = sum([weights[i] for i in candidates]), spare
        for i in candidates:
            extra = min(most - holding[i], max(1, remaining * weights[i] // mass), spare)
            holding[i] = holding[i] + extra
            spare = spare - extra
    return np.array(holding)


def scatter_about(own_key, shape, spread, reach, shards=(), kind=jnp.bfloat16):
    drawn = spread * jax.random.normal(own_key, shape, jnp.float32)
    if shards:
        drawn = drawn * shard_levels(own_key, shape, shards, -0.22, 0.18)
    return jnp.clip(drawn, -reach, reach).astype(kind)


def setup_inputs(seed: int = 0) -> dict:
    streams_of = jax.random.split(jax.random.key(seed), 11)
    raw_tiles = scatter_about(streams_of[0], (4, ROWS, COLS), 1.0, 6.0, ((1, 128),))
    stem_weight = scatter_about(streams_of[1], (STEM_CH, 4, 3, 3), 36 ** -0.5, 1.0)
    embed_weight = scatter_about(streams_of[2], (PATCH_DIM, D), PATCH_DIM ** -0.5, 0.21875)
    norm_gain = jnp.clip(1.0 + 0.18 * jax.random.normal(streams_of[3], (D,), jnp.float32), 0.1, 1.9)
    router_weight = scatter_about(streams_of[4], (D, EXPERTS), D ** -0.5, 0.1875)
    w_gate = scatter_about(streams_of[5], (EXPERTS, D, FF), D ** -0.5, 0.1875, ((0, 32), (2, 4)))
    w_up = scatter_about(streams_of[6], (EXPERTS, D, FF), D ** -0.5, 0.1875, ((0, 32), (2, 4)))
    w_down = scatter_about(streams_of[7], (EXPERTS, FF, D), FF ** -0.5, 0.09375, ((0, 32), (1, 4)))
    routes_keys = jax.random.split(jax.random.fold_in(streams_of[8], 1), TOKENS // TOK_DEV)
    routes_turns = jax.random.permutation(jax.random.fold_in(streams_of[8], 3), TOKENS // TOK_DEV)
    routes = jax.vmap(lambda own, number: assign_block(jax.random.fold_in(streams_of[8], 2), own, number, TOK_DEV, EXPERTS, TOP, CAP, 2))(routes_keys, routes_turns).reshape((TOKENS, TOP))
    cotangent = scatter_about(streams_of[9], (TOKENS, D), 1.0, 6.0, ((0, 128),))
    return {"raw_tiles": raw_tiles, "stem_weight": stem_weight, "embed_weight": embed_weight, "norm_gain": norm_gain, "router_weight": router_weight, "w_gate": w_gate, "w_up": w_up, "w_down": w_down, "routes": routes, "cotangent": cotangent}


GELU_C = 0.7978845608028654
GELU_A = 0.044715
EPSILON = 1e-06

def gelu_value(preact):
    tanh_v = jnp.tanh(GELU_C * (preact + GELU_A * preact * preact * preact))
    return 0.5 * preact * (1.0 + tanh_v)

def gelu_slope(preact):
    tanh_v = jnp.tanh(GELU_C * (preact + GELU_A * preact * preact * preact))
    return 0.5 * (1.0 + tanh_v) + 0.5 * preact * (1.0 - tanh_v * tanh_v) * GELU_C * (1.0 + 3.0 * GELU_A * preact * preact)

def stem_stack(padded):
    pixel_rows = padded.shape[1] - 2
    pixel_cols = padded.shape[2]
    widened = jnp.pad(padded, ((0, 0), (0, 0), (1, 1)))
    pieces = [widened[:, row_step:row_step + pixel_rows, col_step:col_step + pixel_cols] for row_step in range(3) for col_step in range(3)]
    stacked = jnp.stack(pieces, axis=1)
    return stacked.reshape(36, pixel_rows * pixel_cols)

def patchify(feature_b, pixel_rows, pixel_cols):
    channels = feature_b.shape[0]
    patch_grid = feature_b.reshape(channels, pixel_rows // PATCH, PATCH, pixel_cols // PATCH, PATCH)
    patch_grid = patch_grid.transpose(1, 3, 0, 2, 4)
    return patch_grid.reshape(pixel_rows // PATCH * (pixel_cols // PATCH), channels * PATCH * PATCH)

def unpatchify(patch_cot, pixel_rows, pixel_cols, channels):
    patch_grid = patch_cot.reshape(pixel_rows // PATCH, pixel_cols // PATCH, channels, PATCH, PATCH)
    patch_grid = patch_grid.transpose(2, 0, 3, 1, 4)
    return patch_grid.reshape(channels, pixel_rows * pixel_cols)

def front(padded, stem_weight, embed_weight, norm_gain):
    pixel_rows = padded.shape[1] - 2
    pixel_cols = padded.shape[2]
    stacked = stem_stack(padded)
    kernel = stem_weight.reshape(stem_weight.shape[0], 36)
    preact = jnp.dot(kernel, stacked, preferred_element_type=jnp.float32)
    feature_b = gelu_value(preact).astype(jnp.bfloat16)
    patches_b = patchify(feature_b, pixel_rows, pixel_cols)
    embedded = jnp.dot(patches_b, embed_weight, preferred_element_type=jnp.float32)
    inv_rms = lax.rsqrt(lax.optimization_barrier(jnp.mean(embedded * embedded, axis=-1, keepdims=True)) + EPSILON)
    hidden_b = (embedded * inv_rms * norm_gain).astype(jnp.bfloat16)
    return (stacked, preact, patches_b, embedded, inv_rms, hidden_b)

def back_front(stacked, preact, patches_b, embedded, inv_rms, norm_gain, embed_weight, upstream, pixel_rows, pixel_cols):
    normed = embedded * inv_rms
    scaled = upstream * norm_gain
    embed_in = inv_rms * (scaled - normed * lax.optimization_barrier(jnp.mean(scaled * normed, axis=-1, keepdims=True)))
    gain_part = lax.optimization_barrier(jnp.sum(upstream * normed, axis=0))
    embed_cot = embed_in.astype(jnp.bfloat16)
    embed_part = jnp.dot(patches_b.T, embed_cot, preferred_element_type=jnp.float32)
    patch_cot = jnp.dot(embed_cot, embed_weight.T, preferred_element_type=jnp.float32)
    feature_cot = unpatchify(patch_cot, pixel_rows, pixel_cols, preact.shape[0])
    preact_cot = (feature_cot * gelu_slope(preact)).astype(jnp.bfloat16)
    stem_part = jnp.dot(preact_cot, stacked.T, preferred_element_type=jnp.float32)
    return (gain_part, embed_part, stem_part)

def slot_index(route_rows, experts, capacity):
    chosen = route_rows.reshape(-1)
    onehot = (chosen[:, None] == jnp.arange(experts, dtype=jnp.int32)[None, :]).astype(jnp.int32)
    before = jnp.cumsum(onehot, axis=0) - onehot
    slot_pos = lax.optimization_barrier(jnp.sum(before * onehot, axis=1))
    return (chosen * capacity + slot_pos).astype(jnp.int32)

def gate_scores(logits, routes):
    picked = jnp.take_along_axis(logits, routes, axis=1)
    return jax.nn.sigmoid(picked)

def router_cot(score_grad, gate_score, routes, experts):
    local_grad = score_grad * gate_score * (1.0 - gate_score)
    chosen_hot = (routes[:, :, None] == jnp.arange(experts, dtype=jnp.int32)[None, None, :]).astype(jnp.float32)
    return lax.optimization_barrier(jnp.sum(chosen_hot * local_grad[:, :, None], axis=1)).astype(jnp.bfloat16)

def expert_pass(operands):
    slot_rows, slot_cots, gate_matrix, up_matrix, down_matrix = operands
    gate_proj = jnp.dot(slot_rows, gate_matrix, preferred_element_type=jnp.float32)
    up_proj = jnp.dot(slot_rows, up_matrix, preferred_element_type=jnp.float32)
    sigmoid_gate = jax.nn.sigmoid(gate_proj)
    activated = gate_proj * sigmoid_gate
    hidden_act = (activated * up_proj).astype(jnp.bfloat16)
    expert_out = jnp.dot(hidden_act, down_matrix, preferred_element_type=jnp.float32).astype(jnp.bfloat16)
    act_cot = jnp.dot(slot_cots, down_matrix.T, preferred_element_type=jnp.float32)
    gate_cot = (act_cot * up_proj * (sigmoid_gate * (1.0 + gate_proj * (1.0 - sigmoid_gate)))).astype(jnp.bfloat16)
    up_cot = (act_cot * activated).astype(jnp.bfloat16)
    grad_gate = jnp.dot(slot_rows.T, gate_cot, preferred_element_type=jnp.float32)
    grad_up = jnp.dot(slot_rows.T, up_cot, preferred_element_type=jnp.float32)
    grad_down = jnp.dot(hidden_act.T, slot_cots, preferred_element_type=jnp.float32)
    slot_cot = jnp.dot(gate_cot, gate_matrix.T, preferred_element_type=jnp.float32) + jnp.dot(up_cot, up_matrix.T, preferred_element_type=jnp.float32)
    return (expert_out, slot_cot.astype(jnp.bfloat16), grad_gate, grad_up, grad_down)

def reference(raw_tiles, stem_weight, embed_weight, norm_gain, router_weight, w_gate, w_up, w_down, routes, cotangent):
    devices = N_DE * N_TP
    experts = EXP_DEV * N_DE
    capacity = CAP
    model_width = cotangent.shape[1]
    pixel_rows = raw_tiles.shape[1]
    pixel_cols = raw_tiles.shape[2]
    padded = jnp.pad(raw_tiles, ((0, 0), (1, 1), (0, 0)))
    stacked, preact, patches_b, embedded, inv_rms, hidden_b = front(padded, stem_weight, embed_weight, norm_gain)
    logits = jnp.dot(hidden_b, router_weight, preferred_element_type=jnp.float32)
    gate_score = gate_scores(logits, routes)
    slot_flat = jax.vmap(lambda route_rows: slot_index(route_rows, experts, capacity))(routes.reshape(devices, TOK_DEV, TOP))
    hidden_pairs = jnp.repeat(hidden_b, TOP, axis=0).reshape(devices, TOK_DEV * TOP, model_width)
    cot_pairs = jnp.repeat(cotangent.astype(jnp.float32), TOP, axis=0)
    out_cot = (gate_score.reshape(-1, 1) * cot_pairs).astype(jnp.bfloat16).reshape(devices, TOK_DEV * TOP, model_width)
    device_ids = jnp.arange(devices, dtype=jnp.int32)[:, None]
    blank_slots = jnp.zeros((devices, experts * capacity, model_width), jnp.bfloat16)
    sent_rows = blank_slots.at[device_ids, slot_flat].set(hidden_pairs)
    sent_cots = blank_slots.at[device_ids, slot_flat].set(out_cot)

    def by_expert(buffer):
        return buffer.reshape(devices, experts, capacity, model_width).transpose(1, 0, 2, 3).reshape(experts, devices * capacity, model_width)

    def to_source(buffer):
        return buffer.reshape(experts, devices, capacity, model_width).transpose(1, 0, 2, 3).reshape(devices, experts * capacity, model_width)
    expert_out, slot_cot, grad_gate, grad_up, grad_down = lax.map(expert_pass, (by_expert(sent_rows), by_expert(sent_cots), w_gate, w_up, w_down))
    pick_rows = jax.vmap(lambda table, index: jnp.take(table, index, axis=0))
    out_pairs = pick_rows(to_source(expert_out), slot_flat).reshape(-1, model_width)
    cot_back = pick_rows(to_source(slot_cot), slot_flat).reshape(-1, model_width)
    out_wide = out_pairs.astype(jnp.float32)
    expert_mix = lax.optimization_barrier(jnp.sum((gate_score.reshape(-1, 1) * out_wide).reshape(-1, TOP, model_width), axis=1)).astype(jnp.bfloat16)
    score_grad = lax.optimization_barrier(jnp.sum(cot_pairs * out_wide, axis=-1)).reshape(-1, TOP)
    logit_cot = router_cot(score_grad, gate_score, routes, experts)
    grad_router = jnp.dot(hidden_b.T, logit_cot, preferred_element_type=jnp.float32)
    upstream = lax.optimization_barrier(jnp.sum(cot_back.astype(jnp.float32).reshape(-1, TOP, model_width), axis=1))
    upstream = upstream + jnp.dot(logit_cot, router_weight.T, preferred_element_type=jnp.float32)
    grad_gain, grad_embed, stem_part = back_front(stacked, preact, patches_b, embedded, inv_rms, norm_gain, embed_weight, upstream, pixel_rows, pixel_cols)
    return (expert_mix, grad_gate, grad_up, grad_down, grad_router, grad_gain, grad_embed, stem_part.reshape(stem_weight.shape))
```

```python
import jax
import jax.numpy as jnp
import numpy as np
from jax import lax
from jax.sharding import PartitionSpec as P

PATCH = 4
GELU_C = 0.7978845608028654
GELU_A = 0.044715
EPSILON = 1e-06
BF = jnp.bfloat16
F32 = jnp.float32
PIX = 144
DE = ("xz", "core")
ALL = ("tp", "xz", "core")
DE_TP = ("xz", "core", "tp")
HALF = ("xz", "tp")


def dot(a, b, dims=((1,), (0,))):
    return lax.dot_general(a, b, (dims, ((), ())), preferred_element_type=F32)


def halo_rows(raw):
    count = lax.axis_size(DE_TP)
    forward = [(i, i + 1) for i in range(count - 1)]
    backward = [(target, source) for source, target in forward]
    low = lax.ppermute(raw[:, -1:], DE_TP, forward)
    high = lax.ppermute(raw[:, :1], DE_TP, backward)
    return jnp.concatenate([low, raw, high], axis=1)


def window_rows(padded, tokens):
    chans, rows, cols = padded.shape
    flat = padded.reshape(chans * rows, cols)
    step = lax.broadcasted_iota(jnp.int32, (6, tokens, cols), 0)
    token = lax.broadcasted_iota(jnp.int32, (6, tokens, cols), 1)
    col = lax.broadcasted_iota(jnp.int32, (6, tokens, cols), 2)
    pick = (col == PATCH * token + step - 1).astype(BF)
    out = lax.dot_general(pick, flat, (((2,), (1,)), ((), ())), preferred_element_type=F32)
    return out.transpose(1, 0, 2).reshape(tokens, 6 * chans * rows).astype(BF)


def placement():
    place = np.zeros((6, 4, 6, 16, 4, 3, 3), np.float32)
    for r in range(4):
        for c in range(4):
            for a in range(3):
                for b in range(3):
                    for i in range(4):
                        place[c + b, i, r + a, r * 4 + c, i, a, b] = 1
    return place.reshape(PIX, 16 * 36)


def cell_mask(channels):
    cell = lax.broadcasted_iota(jnp.int32, (16, channels * 16), 0)
    col = lax.broadcasted_iota(jnp.int32, (16, channels * 16), 1)
    return cell == col % 16


def spread(channels):
    chan = lax.broadcasted_iota(jnp.int32, (channels, channels * 16), 0)
    col = lax.broadcasted_iota(jnp.int32, (channels, channels * 16), 1)
    return (chan == col // 16).astype(BF)


def stem_matrix(stem_weight):
    channels = stem_weight.shape[0]
    taps = stem_weight.reshape(channels, 36)
    wide = dot(taps, spread(channels), ((0,), (0,))).astype(BF)
    stack = jnp.where(cell_mask(channels)[:, None, :], wide[None], BF(0))
    return dot(jnp.asarray(placement(), BF), stack.reshape(16 * 36, channels * 16)).astype(BF)


def stem_gather(product):
    channels = product.shape[1] // 16
    cells = dot(jnp.asarray(placement(), BF), product.astype(BF), ((0,), (0,)))
    cells = cells.reshape(16, 36, channels * 16)
    wide = jnp.sum(jnp.where(cell_mask(channels)[:, None, :], cells, 0.0), axis=0)
    return dot(spread(channels), wide.astype(BF), ((1,), (1,)))


def slots_of(route, experts, capacity):
    tokens = route.shape[0]
    hot = (route[:, None] == jnp.arange(experts, dtype=jnp.int32)[None, :]).astype(F32)
    row = lax.broadcasted_iota(jnp.int32, (tokens, tokens), 0)
    col = lax.broadcasted_iota(jnp.int32, (tokens, tokens), 1)
    before = dot((col < row).astype(BF), hot.astype(BF))
    return route * capacity + jnp.sum(before * hot, axis=1).astype(jnp.int32)


def swap(block):
    count = lax.axis_size("core")
    return lax.ppermute(block, "core", [(i, count - 1 - i) for i in range(count)])


def total_over_all(pieces):
    count = pieces.shape[0] // 2
    core = lax.axis_index("core")
    own = lax.dynamic_slice_in_dim(pieces, core * count, count, axis=0)
    other = lax.dynamic_slice_in_dim(pieces, (1 - core) * count, count, axis=0)
    chip = (own.astype(F32) + swap(other).astype(F32)).astype(BF)
    parts = lax.all_to_all(chip, HALF, split_axis=0, concat_axis=0, tiled=True)
    total = jnp.sum(parts.astype(F32), axis=0).astype(BF)
    copies = jnp.broadcast_to(total[None], parts.shape)
    mine = lax.all_to_all(copies, HALF, split_axis=0, concat_axis=0, tiled=True)
    theirs = swap(mine)
    first = jnp.where(core == 0, mine, theirs)
    second = jnp.where(core == 0, theirs, mine)
    return jnp.concatenate([first, second], axis=0).astype(F32)


def local(
    raw_tiles,
    stem_weight,
    embed_weight,
    norm_gain,
    router_weight,
    w_gate,
    w_up,
    w_down,
    routes,
    cotangent,
):
    tokens, width = cotangent.shape
    owners = lax.axis_size(DE)
    members = lax.axis_size("tp")
    devices = owners * members
    experts = owners
    capacity = 2 * tokens // experts
    slots = experts * capacity
    total = devices * capacity
    w_gate, w_up, w_down = w_gate[0], w_up[0], w_down[0]

    slot_of = slots_of(routes[:, 0], experts, capacity)
    selector = (slot_of[None, :] == jnp.arange(slots, dtype=jnp.int32)[:, None]).astype(BF)
    sent_cots = dot(selector, cotangent).astype(BF)
    moved = lax.all_to_all(
        sent_cots.reshape(experts, capacity, width), DE, split_axis=0, concat_axis=0, tiled=True
    )
    cots = lax.all_gather(moved, "tp", axis=0, tiled=True).reshape(total, width)

    windows = window_rows(halo_rows(raw_tiles), tokens)
    sent_windows = dot(selector, windows).astype(BF).reshape(1, experts, capacity, PIX)
    sent_windows = jnp.broadcast_to(sent_windows, (members, experts, capacity, PIX))
    cells = lax.all_to_all(
        sent_windows.reshape(devices, capacity, PIX), ALL, split_axis=0, concat_axis=0, tiled=True
    ).reshape(total, PIX)

    conv = stem_matrix(stem_weight)
    preact = dot(cells, conv)
    tanh_v = jnp.tanh(GELU_C * (preact + GELU_A * preact * preact * preact))
    patches = (0.5 * preact * (1.0 + tanh_v)).astype(BF)
    embedded = dot(patches, embed_weight)
    inv_rms = lax.rsqrt(jnp.mean(embedded * embedded, axis=-1, keepdims=True) + EPSILON)
    normed = embedded * inv_rms
    hidden = (normed * norm_gain).astype(BF)
    expert = lax.axis_index(DE)
    router_row = lax.dynamic_slice_in_dim(router_weight, expert, 1, axis=1).reshape(1, width)
    logit = jnp.sum(hidden.astype(F32) * router_row.astype(F32), axis=1, keepdims=True)
    score = jax.nn.sigmoid(logit)

    gate_proj = dot(hidden, w_gate)
    up_proj = dot(hidden, w_up)
    sigmoid_gate = jax.nn.sigmoid(gate_proj)
    activated = gate_proj * sigmoid_gate
    hidden_act = (activated * up_proj).astype(BF)
    out_part = dot(hidden_act, w_down).astype(BF)
    out_share = lax.psum_scatter(out_part, "tp", scatter_dimension=0, tiled=True)
    score_share = lax.dynamic_slice_in_dim(score, lax.axis_index("tp") * slots, slots, axis=0)
    mixed = (out_share.astype(F32) * score_share).astype(BF).reshape(experts, capacity, width)
    returned = lax.all_to_all(mixed, DE, split_axis=0, concat_axis=0, tiled=True)
    expert_mix = dot(selector, returned.reshape(slots, width), ((0,), (0,))).astype(BF)

    act_raw = dot(cots, w_down, ((1,), (1,)))
    score_grad = jnp.sum(hidden_act.astype(F32) * act_raw, axis=1, keepdims=True)
    logit_cot = score_grad * score * (1.0 - score)
    act_cot = score * act_raw
    gate_cot = (
        act_cot * up_proj * (sigmoid_gate * (1.0 + gate_proj * (1.0 - sigmoid_gate)))
    ).astype(BF)
    up_cot = (act_cot * activated).astype(BF)
    slot_cot = dot(gate_cot, w_gate, ((1,), (1,))) + dot(up_cot, w_up, ((1,), (1,)))
    upstream = slot_cot + logit_cot * router_row.astype(F32)
    scaled = upstream * norm_gain
    embed_cot = (
        inv_rms * (scaled - normed * jnp.mean(scaled * normed, axis=-1, keepdims=True))
    ).astype(BF)
    gain_part = jnp.sum(upstream * normed, axis=0)
    router_part = jnp.sum(hidden.astype(F32) * logit_cot, axis=0)
    embed_part = dot(patches, embed_cot, ((0,), (0,)))
    feature_cot = dot(embed_cot, embed_weight, ((1,), (1,)))
    slope = 0.5 * (1.0 + tanh_v) + 0.5 * preact * (1.0 - tanh_v * tanh_v) * GELU_C * (
        1.0 + 3.0 * GELU_A * preact * preact
    )
    preact_cot = (feature_cot * slope).astype(BF)
    stem_part = stem_gather(dot(cells, preact_cot, ((0,), (0,))))

    main = embed_part.astype(BF).reshape(16, 48, 8, 128).transpose(0, 2, 1, 3).reshape(128, 48, 128)
    own_expert = jnp.arange(experts, dtype=jnp.int32)[:, None] == expert
    router_rows = jnp.where(own_expert, router_part[None, :], 0.0)
    small = jnp.concatenate([router_rows.reshape(-1), gain_part, stem_part.reshape(-1)]).astype(BF)
    small = jnp.pad(small, (0, 128 * 1024 - small.shape[0])).reshape(128, 8, 128)
    summed = total_over_all(jnp.concatenate([main, small], axis=1))
    embed_total = summed[:, :48].reshape(16, 8, 48, 128).transpose(0, 2, 1, 3).reshape(768, width)
    flat = summed[:, 48:].reshape(-1)
    router_total = flat[: experts * width].reshape(experts, width).T
    gain_total = flat[experts * width : experts * width + width]
    stem_total = flat[experts * width + width : experts * width + width + stem_weight.size]

    grad_gate = dot(hidden, gate_cot, ((0,), (0,)))
    grad_up = dot(hidden, up_cot, ((0,), (0,)))
    out_cot = (score * cots.astype(F32)).astype(BF)
    grad_down = dot(hidden_act, out_cot, ((0,), (0,)))
    return (
        expert_mix,
        grad_gate[None],
        grad_up[None],
        grad_down[None],
        router_total,
        gain_total,
        embed_total,
        stem_total.reshape(stem_weight.shape),
    )


def solution(mesh):
    owners, members = mesh.devices.shape
    fine = jax.sharding.Mesh(mesh.devices.reshape(owners // 2, 2, members), ("xz", "core", "tp"))
    return jax.shard_map(
        local,
        mesh=fine,
        in_specs=(
            P(None, DE_TP, None),
            P(),
            P(),
            P(),
            P(),
            P(DE, None, "tp"),
            P(DE, None, "tp"),
            P(DE, "tp", None),
            P(DE_TP, None),
            P(DE_TP, None),
        ),
        out_specs=(
            P(DE_TP, None),
            P(DE, None, "tp"),
            P(DE, None, "tp"),
            P(DE, "tp", None),
            P(),
            P(),
            P(),
            P(),
        ),
        check_vma=False,
    )
```

```python
import jax
import jax.numpy as jnp
import numpy as np
from jax import lax
from jax.experimental import pallas as pl
from jax.experimental.pallas import tpu as pltpu
from jax.sharding import PartitionSpec as P

PATCH = 4
GELU_C = 0.7978845608028654
GELU_A = 0.044715
EPSILON = 1e-06
BF = jnp.bfloat16
F32 = jnp.float32
PIX = 144
DE = ("xz", "core")
ALL = ("tp", "xz", "core")
DE_TP = ("xz", "core", "tp")
HALF = ("xz", "tp")


def dot(a, b, dims=((1,), (0,))):
    return lax.dot_general(a, b, (dims, ((), ())), preferred_element_type=F32)


def halo_rows(raw):
    count = lax.axis_size(DE_TP)
    forward = [(i, i + 1) for i in range(count - 1)]
    backward = [(target, source) for source, target in forward]
    low = lax.ppermute(raw[:, -1:], DE_TP, forward)
    high = lax.ppermute(raw[:, :1], DE_TP, backward)
    return jnp.concatenate([low, raw, high], axis=1)


def window_rows(padded, tokens):
    chans, rows, cols = padded.shape
    flat = padded.reshape(chans * rows, cols)
    step = lax.broadcasted_iota(jnp.int32, (6, tokens, cols), 0)
    token = lax.broadcasted_iota(jnp.int32, (6, tokens, cols), 1)
    col = lax.broadcasted_iota(jnp.int32, (6, tokens, cols), 2)
    pick = (col == PATCH * token + step - 1).astype(BF)
    out = lax.dot_general(pick, flat, (((2,), (1,)), ((), ())), preferred_element_type=F32)
    return out.transpose(1, 0, 2).reshape(tokens, 6 * chans * rows).astype(BF)


def placement():
    place = np.zeros((6, 4, 6, 16, 4, 3, 3), np.float32)
    for r in range(4):
        for c in range(4):
            for a in range(3):
                for b in range(3):
                    for i in range(4):
                        place[c + b, i, r + a, r * 4 + c, i, a, b] = 1
    return place.reshape(PIX, 16 * 36)


TAPS = 40


def placement_rows():
    place = placement().T.reshape(16, 36, PIX)
    return np.pad(place, ((0, 0), (0, TAPS - 36), (0, 0))).reshape(16 * TAPS, PIX)


def front_kernel(
    cells_ref, conv_ref, embed_ref, gain_ref, router_ref, gate_ref, up_ref, down_ref,
    patches_ref, slope_ref, hidden_ref, normed_ref, inv_ref, score_ref, act_ref, silu_ref, fac_ref, out_ref,
):
    preact = dot(cells_ref[...], conv_ref[...])
    square = preact * preact
    tanh_v = jnp.tanh(GELU_C * (preact + GELU_A * square * preact))
    half = 0.5 * (1.0 + tanh_v)
    patches = (preact * half).astype(BF)
    patches_ref[...] = patches
    slope_ref[...] = half + 0.5 * preact * (1.0 - tanh_v * tanh_v) * GELU_C * (
        1.0 + 3.0 * GELU_A * square
    )
    embedded = dot(patches, embed_ref[...])
    inv_rms = lax.rsqrt(jnp.mean(embedded * embedded, axis=-1, keepdims=True) + EPSILON)
    inv_ref[...] = inv_rms
    normed = embedded * inv_rms
    normed_ref[...] = normed
    hidden = (normed * gain_ref[...]).astype(BF)
    hidden_ref[...] = hidden
    logit = jnp.sum(hidden.astype(F32) * router_ref[...], axis=1, keepdims=True)
    score_ref[...] = jax.nn.sigmoid(logit)
    gate_proj = dot(hidden, gate_ref[...])
    up_proj = dot(hidden, up_ref[...])
    sigmoid_gate = jax.nn.sigmoid(gate_proj)
    activated = gate_proj * sigmoid_gate
    silu_ref[...] = activated
    fac_ref[...] = up_proj * (sigmoid_gate * (1.0 + gate_proj * (1.0 - sigmoid_gate)))
    hidden_act = (activated * up_proj).astype(BF)
    act_ref[...] = hidden_act
    out_ref[...] = dot(hidden_act, down_ref[...]).astype(BF)


def whole(shape):
    return pl.BlockSpec(shape, lambda i: (0,) * len(shape), pipeline_mode=pl.Buffered(1))


def rows_of(block, width):
    return pl.BlockSpec((block, width), lambda i: (i, 0))


def front(cells, conv, embed_weight, gain, router_row, w_gate, w_up, w_down):
    total = cells.shape[0]
    pixels = conv.shape[1]
    width = embed_weight.shape[1]
    units = w_gate.shape[1]
    block = 256
    sizes = (
        (pixels, BF), (pixels, F32), (width, BF), (width, F32), (1, F32), (1, F32),
        (units, BF), (units, F32), (units, F32), (width, BF),
    )
    return pl.pallas_call(
        front_kernel,
        grid=(total // block,),
        in_specs=[
            rows_of(block, PIX), whole(conv.shape), whole(embed_weight.shape), whole(gain.shape),
            whole(router_row.shape), whole(w_gate.shape), whole(w_up.shape), whole(w_down.shape),
        ],
        out_specs=[rows_of(block, size) for size, _ in sizes],
        out_shape=[jax.ShapeDtypeStruct((total, size), kind) for size, kind in sizes],
        compiler_params=pltpu.CompilerParams(vmem_limit_bytes=48 << 20),
        cost_estimate=pl.CostEstimate(flops=8 << 30, bytes_accessed=32 << 20, transcendentals=0),
    )(cells, conv, embed_weight, gain, router_row, w_gate, w_up, w_down)


def back_kernel(
    expert_ref, cots_ref, silu_ref, fac_ref, act_ref, score_ref, normed_ref, inv_ref, hidden_ref, slope_ref,
    patches_ref, cells_ref, place_ref, router_ref, gain_ref, embed_ref, gate_ref, up_ref, down_ref,
    gate_cot_ref, up_cot_ref, out_cot_ref, pieces_ref,
    embed_cot_ref, preact_cot_ref, sums_ref,
):
    step = pl.program_id(0)
    block = cots_ref.shape[0]
    rows = pl.ds(pl.multiple_of(step * block, block), block)
    cot = cots_ref[...]
    act_raw = dot(cot, down_ref[...], ((1,), (1,)))
    score = score_ref[...]
    score_grad = jnp.sum(act_ref[...].astype(F32) * act_raw, axis=1, keepdims=True)
    logit_cot = score_grad * score * (1.0 - score)
    out_cot_ref[...] = (score * cot.astype(F32)).astype(BF)
    act_cot = score * act_raw
    gate_cot = (act_cot * fac_ref[...]).astype(BF)
    up_cot = (act_cot * silu_ref[...]).astype(BF)
    gate_cot_ref[...] = gate_cot
    up_cot_ref[...] = up_cot
    slot_cot = dot(gate_cot, gate_ref[...], ((1,), (1,))) + dot(up_cot, up_ref[...], ((1,), (1,)))
    upstream = slot_cot + logit_cot * router_ref[...]
    normed = normed_ref[...]
    scaled = upstream * gain_ref[...]
    product = upstream * normed
    mean = jnp.mean(product * gain_ref[...], axis=-1, keepdims=True)
    embed_cot = (inv_ref[...] * (scaled - normed * mean)).astype(BF)
    embed_cot_ref[rows, :] = embed_cot

    @pl.when(step == 0)
    def _():
        sums_ref[...] = jnp.zeros_like(sums_ref)

    sums_ref[0:1, :] += jnp.sum(hidden_ref[...].astype(F32) * logit_cot, axis=0, keepdims=True)
    sums_ref[1:2, :] += jnp.sum(product, axis=0, keepdims=True)
    feature_cot = dot(embed_cot, embed_ref[...], ((1,), (1,)))
    preact_cot_ref[rows, :] = (feature_cot * slope_ref[...]).astype(BF)

    @pl.when(step == pl.num_programs(0) - 1)
    def _():
        tall, lanes = 48, 128
        embed_part = dot(patches_ref[...], embed_cot_ref[...], ((0,), (0,)))
        across = embed_part.shape[1] // lanes
        for a in range(embed_part.shape[0] // tall):
            for b in range(across):
                pieces_ref[a * across + b, 0:tall, :] = embed_part[
                    a * tall : a * tall + tall, b * lanes : b * lanes + lanes
                ]
        product_sum = dot(cells_ref[...], preact_cot_ref[...], ((0,), (0,)))
        taps = dot(place_ref[...], product_sum.astype(BF))
        pixels = taps.shape[1]
        col = lax.broadcasted_iota(jnp.int32, (TAPS, pixels), 1)
        wide = jnp.zeros((TAPS, pixels), F32)
        for cell in range(16):
            wide += jnp.where(col % 16 == cell, taps[cell * TAPS : cell * TAPS + TAPS], 0.0)
        chan = lax.broadcasted_iota(jnp.int32, (lanes, pixels), 0)
        group = lax.broadcasted_iota(jnp.int32, (lanes, pixels), 1)
        stem = dot(wide.astype(BF), (chan == group // 16).astype(BF), ((1,), (1,)))

        def folded(row):
            return jnp.concatenate(
                [row[:, k * lanes : k * lanes + lanes] for k in range(across)], axis=0
            )

        router = folded(sums_ref[0:1, :])
        for e in range(32):
            pieces_ref[e, tall:, :] = jnp.where(expert_ref[0] == e, router, 0.0)
        pieces_ref[32, tall:, :] = folded(sums_ref[1:2, :])
        for k in range(5):
            pieces_ref[33 + k, tall:, :] = stem[8 * k : 8 * k + 8]
        for k in range(38, pieces_ref.shape[0]):
            pieces_ref[k, tall:, :] = jnp.zeros((8, lanes), F32)


def back(expert, cots, saved, cells, router_row, gain, embed_weight, w_gate, w_up, w_down):
    patches, slope, hidden, normed, inv_rms, score, hidden_act, silu, fac = saved
    total, width = cots.shape
    units = w_gate.shape[1]
    pixels = patches.shape[1]
    block = 256
    place = jnp.asarray(placement_rows(), BF)
    ins = (
        (expert, pl.BlockSpec(memory_space=pltpu.SMEM)),
        (cots, rows_of(block, width)),
        (silu, rows_of(block, units)),
        (fac, rows_of(block, units)),
        (hidden_act, rows_of(block, units)),
        (score, rows_of(block, 1)),
        (normed, rows_of(block, width)),
        (inv_rms, rows_of(block, 1)),
        (hidden, rows_of(block, width)),
        (slope, rows_of(block, pixels)),
        (patches, whole(patches.shape)),
        (cells, whole(cells.shape)),
        (place, whole(place.shape)),
        (router_row, whole(router_row.shape)),
        (gain, whole(gain.shape)),
        (embed_weight, whole(embed_weight.shape)),
        (w_gate, whole(w_gate.shape)),
        (w_up, whole(w_up.shape)),
        (w_down, whole(w_down.shape)),
    )
    return pl.pallas_call(
        back_kernel,
        grid=(total // block,),
        in_specs=[spec for _, spec in ins],
        out_specs=[rows_of(block, units), rows_of(block, units), rows_of(block, width), whole((128, 56, 128))],
        out_shape=[
            jax.ShapeDtypeStruct((total, units), BF),
            jax.ShapeDtypeStruct((total, units), BF),
            jax.ShapeDtypeStruct((total, width), BF),
            jax.ShapeDtypeStruct((128, 56, 128), F32),
        ],
        scratch_shapes=[
            pltpu.VMEM((total, width), BF),
            pltpu.VMEM((total, pixels), BF),
            pltpu.VMEM((8, width), F32),
        ],
        compiler_params=pltpu.CompilerParams(vmem_limit_bytes=56 << 20),
        cost_estimate=pl.CostEstimate(flops=10 << 30, bytes_accessed=36 << 20, transcendentals=0),
    )(*[x for x, _ in ins])


def finish_kernel(core_ref, mine_ref, theirs_ref, embed_ref, router_ref, gain_ref, stem_ref):
    first = core_ref[0] == 0
    count = mine_ref.shape[0]
    tall, lanes = 48, 128
    across = embed_ref.shape[1] // lanes

    def piece(p):
        near = mine_ref[p % count].astype(F32)
        far = theirs_ref[p % count].astype(F32)
        return jnp.where(first, near, far) if p < count else jnp.where(first, far, near)

    experts = router_ref.shape[1]
    rows = []
    for p in range(2 * count):
        value = piece(p)
        a, b = p // across, p % across
        embed_ref[a * tall : a * tall + tall, b * lanes : b * lanes + lanes] = value[:tall]
        if p < experts:
            rows.append(value[tall:])
        elif p == experts:
            gain_ref[...] = value[tall:]
        elif p < experts + 6:
            k = p - experts - 1
            stem_ref[8 * k : 8 * k + 8, :] = value[tall:]
    for k in range(across):
        block = jnp.concatenate([row[k : k + 1] for row in rows], axis=0)
        router_ref[k * lanes : k * lanes + lanes, :] = block.T


def finish(core, mine, theirs, pixels, width, experts):
    return pl.pallas_call(
        finish_kernel,
        in_specs=[
            pl.BlockSpec(memory_space=pltpu.SMEM),
            pl.BlockSpec(memory_space=pltpu.VMEM),
            pl.BlockSpec(memory_space=pltpu.VMEM),
        ],
        out_specs=[pl.BlockSpec(memory_space=pltpu.VMEM)] * 4,
        out_shape=[
            jax.ShapeDtypeStruct((pixels, width), F32),
            jax.ShapeDtypeStruct((width, experts), F32),
            jax.ShapeDtypeStruct((8, 128), F32),
            jax.ShapeDtypeStruct((TAPS, 128), F32),
        ],
        compiler_params=pltpu.CompilerParams(vmem_limit_bytes=32 << 20),
        cost_estimate=pl.CostEstimate(flops=1 << 20, bytes_accessed=6 << 20, transcendentals=0),
    )(core, mine, theirs)


def cell_mask(channels):
    cell = lax.broadcasted_iota(jnp.int32, (16, channels * 16), 0)
    col = lax.broadcasted_iota(jnp.int32, (16, channels * 16), 1)
    return cell == col % 16


def spread(channels):
    chan = lax.broadcasted_iota(jnp.int32, (channels, channels * 16), 0)
    col = lax.broadcasted_iota(jnp.int32, (channels, channels * 16), 1)
    return (chan == col // 16).astype(BF)


def stem_matrix(stem_weight):
    channels = stem_weight.shape[0]
    taps = stem_weight.reshape(channels, 36)
    wide = dot(taps, spread(channels), ((0,), (0,))).astype(BF)
    stack = jnp.where(cell_mask(channels)[:, None, :], wide[None], BF(0))
    return dot(jnp.asarray(placement(), BF), stack.reshape(16 * 36, channels * 16)).astype(BF)


def slots_of(route, experts, capacity):
    tokens = route.shape[0]
    hot = (route[:, None] == jnp.arange(experts, dtype=jnp.int32)[None, :]).astype(F32)
    row = lax.broadcasted_iota(jnp.int32, (tokens, tokens), 0)
    col = lax.broadcasted_iota(jnp.int32, (tokens, tokens), 1)
    before = dot((col < row).astype(BF), hot.astype(BF))
    return route * capacity + jnp.sum(before * hot, axis=1).astype(jnp.int32)


def swap(block):
    count = lax.axis_size("core")
    return lax.ppermute(block, "core", [(i, count - 1 - i) for i in range(count)])


def total_over_all(pieces, beside):
    count = pieces.shape[0] // 2
    core = lax.axis_index("core")
    own = lax.dynamic_slice_in_dim(pieces, core * count, count, axis=0)
    other = lax.dynamic_slice_in_dim(pieces, (1 - core) * count, count, axis=0)
    chip = (own + swap(other.astype(BF)).astype(F32)).astype(BF)
    parts = lax.all_to_all(chip, HALF, split_axis=0, concat_axis=0, tiled=True)
    parts, done = lax.optimization_barrier((parts, beside(chip)))
    total = jnp.sum(parts.astype(F32), axis=0).astype(BF)
    copies = jnp.broadcast_to(total[None], parts.shape)
    mine = lax.all_to_all(copies, HALF, split_axis=0, concat_axis=0, tiled=True)
    theirs = swap(mine)
    return mine, theirs, done


def local(
    raw_tiles,
    stem_weight,
    embed_weight,
    norm_gain,
    router_weight,
    w_gate,
    w_up,
    w_down,
    routes,
    cotangent,
):
    tokens, width = cotangent.shape
    owners = lax.axis_size(DE)
    members = lax.axis_size("tp")
    devices = owners * members
    experts = owners
    capacity = 2 * tokens // experts
    slots = experts * capacity
    total = devices * capacity
    w_gate, w_up, w_down = w_gate[0], w_up[0], w_down[0]

    slot_of = slots_of(routes[:, 0], experts, capacity)
    selector = (slot_of[None, :] == jnp.arange(slots, dtype=jnp.int32)[:, None]).astype(BF)
    sent_cots = dot(selector, cotangent).astype(BF)
    moved = lax.all_to_all(
        sent_cots.reshape(experts, capacity, width), DE, split_axis=0, concat_axis=0, tiled=True
    )
    windows = window_rows(halo_rows(raw_tiles), tokens)
    sent_windows = dot(selector, windows).astype(BF).reshape(1, experts, capacity, PIX)
    sent_windows, moved = lax.optimization_barrier((sent_windows, moved))
    sent_windows = jnp.broadcast_to(sent_windows, (members, experts, capacity, PIX))
    cells = lax.all_to_all(
        sent_windows.reshape(devices, capacity, PIX), ALL, split_axis=0, concat_axis=0, tiled=True
    ).reshape(total, PIX)

    cots = lax.all_gather(moved, "tp", axis=0, tiled=True).reshape(total, width)

    conv = stem_matrix(stem_weight)
    expert = lax.axis_index(DE)
    router_row = lax.dynamic_slice_in_dim(router_weight, expert, 1, axis=1).reshape(1, width)
    router_row = router_row.astype(F32)
    gain = norm_gain.reshape(1, width)
    *saved, out_part = front(cells, conv, embed_weight, gain, router_row, w_gate, w_up, w_down)
    hidden, score, hidden_act = saved[2], saved[5], saved[6]
    out_share = lax.psum_scatter(out_part, "tp", scatter_dimension=0, tiled=True)
    score_share = lax.dynamic_slice_in_dim(score, lax.axis_index("tp") * slots, slots, axis=0)
    mixed = (out_share.astype(F32) * score_share).astype(BF).reshape(experts, capacity, width)
    returned = lax.all_to_all(mixed, DE, split_axis=0, concat_axis=0, tiled=True)
    expert_mix = dot(selector, returned.reshape(slots, width), ((0,), (0,))).astype(BF)

    cots, out_part = lax.optimization_barrier((cots, out_part))
    gate_cot, up_cot, out_cot, pieces = back(
        expert.reshape(1), cots, saved, cells, router_row, gain, embed_weight, w_gate, w_up, w_down
    )

    def weight_grads(ready):
        rows, gates, ups, acts, outs, _ = lax.optimization_barrier(
            (hidden, gate_cot, up_cot, hidden_act, out_cot, ready)
        )
        return (
            dot(rows, gates, ((0,), (0,))),
            dot(rows, ups, ((0,), (0,))),
            dot(acts, outs, ((0,), (0,))),
        )

    mine, theirs, grads = total_over_all(pieces, weight_grads)
    core = lax.axis_index("core").reshape(1)
    embed_total, router_total, gain_total, stem_total = finish(
        core, mine, theirs, embed_weight.shape[0], width, experts
    )
    stem_total = stem_total[:36, : stem_weight.shape[0]].T
    return (
        expert_mix,
        grads[0][None],
        grads[1][None],
        grads[2][None],
        router_total,
        gain_total.reshape(width),
        embed_total,
        stem_total.reshape(stem_weight.shape),
    )


def solution(mesh):
    owners, members = mesh.devices.shape
    fine = jax.sharding.Mesh(mesh.devices.reshape(owners // 2, 2, members), ("xz", "core", "tp"))
    return jax.shard_map(
        local,
        mesh=fine,
        in_specs=(
            P(None, DE_TP, None),
            P(),
            P(),
            P(),
            P(),
            P(DE, None, "tp"),
            P(DE, None, "tp"),
            P(DE, "tp", None),
            P(DE_TP, None),
            P(DE_TP, None),
        ),
        out_specs=(
            P(DE_TP, None),
            P(DE, None, "tp"),
            P(DE, None, "tp"),
            P(DE, "tp", None),
            P(),
            P(),
            P(),
            P(),
        ),
        check_vma=False,
    )
```

```python
import jax
import jax.numpy as jnp
import numpy as np
from jax import lax
from jax.experimental import pallas as pl
from jax.experimental.pallas import tpu as pltpu
from jax.sharding import PartitionSpec as P

PATCH = 4
GELU_C = 0.7978845608028654
GELU_A = 0.044715
EPSILON = 1e-06
BF = jnp.bfloat16
F32 = jnp.float32
PIX = 144
DE = ("xz", "core")
ALL = ("tp", "xz", "core")
DE_TP = ("xz", "core", "tp")
HALF = ("xz", "tp")


def dot(a, b, dims=((1,), (0,))):
    return lax.dot_general(a, b, (dims, ((), ())), preferred_element_type=F32)


def halo_rows(raw):
    count = lax.axis_size(DE_TP)
    forward = [(i, i + 1) for i in range(count - 1)]
    backward = [(target, source) for source, target in forward]
    low = lax.ppermute(raw[:, -1:], DE_TP, forward)
    high = lax.ppermute(raw[:, :1], DE_TP, backward)
    return jnp.concatenate([low, raw, high], axis=1)


def window_rows(padded, tokens):
    chans, rows, cols = padded.shape
    flat = padded.reshape(chans * rows, cols)
    step = lax.broadcasted_iota(jnp.int32, (6, tokens, cols), 0)
    token = lax.broadcasted_iota(jnp.int32, (6, tokens, cols), 1)
    col = lax.broadcasted_iota(jnp.int32, (6, tokens, cols), 2)
    pick = (col == PATCH * token + step - 1).astype(BF)
    out = lax.dot_general(pick, flat, (((2,), (1,)), ((), ())), preferred_element_type=F32)
    return out.transpose(1, 0, 2).reshape(tokens, 6 * chans * rows).astype(BF)


def placement():
    place = np.zeros((6, 4, 6, 16, 4, 3, 3), np.float32)
    for r in range(4):
        for c in range(4):
            for a in range(3):
                for b in range(3):
                    for i in range(4):
                        place[c + b, i, r + a, r * 4 + c, i, a, b] = 1
    return place.reshape(PIX, 16 * 36)


TAPS = 40


def placement_rows():
    place = placement().T.reshape(16, 36, PIX)
    return np.pad(place, ((0, 0), (0, TAPS - 36), (0, 0))).reshape(16 * TAPS, PIX)


VMEM = pl.BlockSpec(memory_space=pltpu.VMEM)
SMEM = pl.BlockSpec(memory_space=pltpu.SMEM)
HBM = pl.BlockSpec(memory_space=pl.ANY)
ROWS = 256
TALL, LANES = 48, 128


def folded(row):
    return jnp.concatenate([row[:, k : k + LANES] for k in range(0, row.shape[1], LANES)], axis=0)


def layer_kernel(
    place_at_ref, gain_ref, router_ref, moved_hbm, conv_hbm, embed_hbm, gate_hbm, up_hbm, down_hbm, place_hbm,
    out_hbm, hidden_hbm, act_hbm, gate_cot_hbm, up_cot_hbm, out_cot_hbm, own_ref, other_ref,
    cells_ref, conv_ref, embed_ref, gate_ref, up_ref, down_ref, cots_ref, place_ref,
    out_ref, hidden_ref, act_ref, gate_cot_ref, up_cot_ref, out_cot_ref, patches_ref, embed_cot_ref, preact_cot_ref,
    in_sems, out_sems,
):
    total, width = cots_ref.shape
    pixels = patches_ref.shape[1]
    across = width // LANES
    arriving = {}
    for k, (name, source, target) in enumerate(
        (
            ("cells", moved_hbm.at[:, width:], cells_ref),
            ("conv", conv_hbm, conv_ref),
            ("embed", embed_hbm, embed_ref),
            ("gate", gate_hbm, gate_ref),
            ("up", up_hbm, up_ref),
            ("down", down_hbm, down_ref),
            ("cots", moved_hbm.at[:, :width], cots_ref),
            ("place", place_hbm, place_ref),
        )
    ):
        arriving[name] = pltpu.make_async_copy(source, target, in_sems.at[k])
        arriving[name].start()

    def need(name):
        if name in arriving:
            arriving.pop(name).wait()

    leaving = []

    def send(rows, k, source, target):
        leaving.append(pltpu.make_async_copy(source.at[rows], target.at[rows], out_sems.at[rows.start // ROWS, k]))
        leaving[-1].start()

    router_sum = jnp.zeros((1, width), F32)
    gain_sum = jnp.zeros((1, width), F32)
    for first in range(0, total, ROWS):
        rows = slice(first, first + ROWS)
        need("cells")
        need("conv")
        preact = dot(cells_ref[rows], conv_ref[...])
        square = preact * preact
        tanh_v = jnp.tanh(GELU_C * (preact + GELU_A * square * preact))
        half = 0.5 * (1.0 + tanh_v)
        patches = (preact * half).astype(BF)
        patches_ref[rows] = patches
        slope = half + 0.5 * preact * (1.0 - tanh_v * tanh_v) * GELU_C * (1.0 + 3.0 * GELU_A * square)
        need("embed")
        embedded = dot(patches, embed_ref[...])
        inv_rms = lax.rsqrt(jnp.mean(embedded * embedded, axis=-1, keepdims=True) + EPSILON)
        normed = embedded * inv_rms
        hidden = (normed * gain_ref[...]).astype(BF)
        hidden_ref[rows] = hidden
        send(rows, 0, hidden_ref, hidden_hbm)
        logit = jnp.sum(hidden.astype(F32) * router_ref[...], axis=1, keepdims=True)
        score = jax.nn.sigmoid(logit)
        need("gate")
        gate_proj = dot(hidden, gate_ref[...])
        need("up")
        up_proj = dot(hidden, up_ref[...])
        sigmoid_gate = jax.nn.sigmoid(gate_proj)
        activated = gate_proj * sigmoid_gate
        factor = up_proj * (sigmoid_gate * (1.0 + gate_proj * (1.0 - sigmoid_gate)))
        hidden_act = (activated * up_proj).astype(BF)
        act_ref[rows] = hidden_act
        send(rows, 1, act_ref, act_hbm)
        need("down")
        out_ref[rows] = (score * dot(hidden_act, down_ref[...])).astype(BF)
        send(rows, 2, out_ref, out_hbm)
        need("cots")
        cot = cots_ref[rows]
        act_raw = dot(cot, down_ref[...], ((1,), (1,)))
        score_grad = jnp.sum(hidden_act.astype(F32) * act_raw, axis=1, keepdims=True)
        logit_cot = score_grad * score * (1.0 - score)
        out_cot_ref[rows] = (score * cot.astype(F32)).astype(BF)
        send(rows, 3, out_cot_ref, out_cot_hbm)
        act_cot = score * act_raw
        gate_cot = (act_cot * factor).astype(BF)
        up_cot = (act_cot * activated).astype(BF)
        gate_cot_ref[rows] = gate_cot
        send(rows, 4, gate_cot_ref, gate_cot_hbm)
        up_cot_ref[rows] = up_cot
        send(rows, 5, up_cot_ref, up_cot_hbm)
        slot_cot = dot(gate_cot, gate_ref[...], ((1,), (1,))) + dot(up_cot, up_ref[...], ((1,), (1,)))
        upstream = slot_cot + logit_cot * router_ref[...]
        scaled = upstream * gain_ref[...]
        mean = jnp.mean(scaled * normed, axis=-1, keepdims=True)
        embed_cot = (inv_rms * (scaled - normed * mean)).astype(BF)
        embed_cot_ref[rows] = embed_cot
        router_sum += jnp.sum(hidden.astype(F32) * logit_cot, axis=0, keepdims=True)
        gain_sum += jnp.sum(upstream * normed, axis=0, keepdims=True)
        feature_cot = dot(embed_cot, embed_ref[...], ((1,), (1,)))
        preact_cot_ref[rows] = (feature_cot * slope).astype(BF)

    product_sum = dot(cells_ref[...], preact_cot_ref[...], ((0,), (0,)))
    need("place")
    taps = dot(place_ref[...], product_sum.astype(BF))
    col = lax.broadcasted_iota(jnp.int32, (TAPS, pixels), 1)
    wide = jnp.zeros((TAPS, pixels), F32)
    for cell in range(16):
        wide += jnp.where(col % 16 == cell, taps[cell * TAPS : cell * TAPS + TAPS], 0.0)
    chan = lax.broadcasted_iota(jnp.int32, (LANES, pixels), 0)
    group = lax.broadcasted_iota(jnp.int32, (LANES, pixels), 1)
    stem = dot(wide.astype(BF), (chan == group // 16).astype(BF), ((1,), (1,)))
    router = folded(router_sum)
    gain = folded(gain_sum)
    expert, core = place_at_ref[0], place_at_ref[1]

    def small(p):
        if p < 32:
            return jnp.where(expert == p, router, 0.0)
        if p == 32:
            return gain
        if p < 38:
            return stem[8 * (p - 33) : 8 * (p - 33) + 8]
        return jnp.zeros((8, LANES), F32)

    part = pixels // 2
    for target, side in ((other_ref, 1 - core), (own_ref, core)):
        columns = pl.ds(pl.multiple_of(side * part, LANES), part)
        embed_part = dot(patches_ref[:, columns], embed_cot_ref[...], ((0,), (0,)))
        for a in range(part // TALL):
            for b in range(across):
                p = a * across + b
                main = embed_part[a * TALL : a * TALL + TALL, b * LANES : b * LANES + LANES]
                rest = jnp.where(side == 0, small(p), 0.0)
                target[p] = jnp.concatenate([main, rest], axis=0).astype(target.dtype)
    for copy in leaving:
        copy.wait()


def layer(place_at, gain, router_row, moved, conv, embed_weight, w_gate, w_up, w_down):
    total = moved.shape[0]
    width = gain.shape[1]
    units = w_gate.shape[1]
    pixels = conv.shape[1]
    place = jnp.asarray(placement_rows(), BF)
    place = jnp.pad(place, ((0, 0), (0, moved.shape[1] - width - PIX)))
    outs = (width, width, units, units, units, width)
    return pl.pallas_call(
        layer_kernel,
        in_specs=[SMEM, VMEM, VMEM] + [HBM] * 7,
        out_specs=[HBM] * len(outs) + [VMEM] * 2,
        out_shape=[jax.ShapeDtypeStruct((total, size), BF) for size in outs]
        + [
            jax.ShapeDtypeStruct((64, TALL + 8, LANES), F32),
            jax.ShapeDtypeStruct((64, TALL + 8, LANES), BF),
        ],
        scratch_shapes=[
            pltpu.VMEM((total, moved.shape[1] - width), BF),
            pltpu.VMEM(conv.shape, BF),
            pltpu.VMEM(embed_weight.shape, BF),
            pltpu.VMEM(w_gate.shape, BF),
            pltpu.VMEM(w_up.shape, BF),
            pltpu.VMEM(w_down.shape, BF),
            pltpu.VMEM((total, width), BF),
            pltpu.VMEM(place.shape, BF),
        ]
        + [pltpu.VMEM((total, size), BF) for size in (*outs, pixels, width, pixels)]
        + [pltpu.SemaphoreType.DMA((8,)), pltpu.SemaphoreType.DMA((total // ROWS, len(outs)))],
        compiler_params=pltpu.CompilerParams(vmem_limit_bytes=52 << 20),
        cost_estimate=pl.CostEstimate(flops=18 << 30, bytes_accessed=30 << 20, transcendentals=0),
    )(place_at, gain, router_row, moved, conv, embed_weight, w_gate, w_up, w_down, place)


def finish_kernel(core_ref, mine_ref, theirs_ref, embed_ref, router_ref, gain_ref, stem_ref):
    first = core_ref[0] == 0
    count = mine_ref.shape[0]
    tall, lanes = 48, 128
    across = embed_ref.shape[1] // lanes

    def piece(p):
        near = mine_ref[p % count].astype(F32)
        far = theirs_ref[p % count].astype(F32)
        return jnp.where(first, near, far) if p < count else jnp.where(first, far, near)

    experts = router_ref.shape[1]
    rows = []
    for p in range(2 * count):
        value = piece(p)
        a, b = p // across, p % across
        embed_ref[a * tall : a * tall + tall, b * lanes : b * lanes + lanes] = value[:tall]
        if p < experts:
            rows.append(value[tall:])
        elif p == experts:
            gain_ref[...] = value[tall:]
        elif p < experts + 6:
            k = p - experts - 1
            stem_ref[8 * k : 8 * k + 8, :] = value[tall:]
    for k in range(across):
        block = jnp.concatenate([row[k : k + 1] for row in rows], axis=0)
        router_ref[k * lanes : k * lanes + lanes, :] = block.T


def finish(core, mine, theirs, pixels, width, experts):
    return pl.pallas_call(
        finish_kernel,
        in_specs=[
            pl.BlockSpec(memory_space=pltpu.SMEM),
            pl.BlockSpec(memory_space=pltpu.VMEM),
            pl.BlockSpec(memory_space=pltpu.VMEM),
        ],
        out_specs=[pl.BlockSpec(memory_space=pltpu.VMEM)] * 4,
        out_shape=[
            jax.ShapeDtypeStruct((pixels, width), F32),
            jax.ShapeDtypeStruct((width, experts), F32),
            jax.ShapeDtypeStruct((8, 128), F32),
            jax.ShapeDtypeStruct((TAPS, 128), F32),
        ],
        compiler_params=pltpu.CompilerParams(vmem_limit_bytes=32 << 20),
        cost_estimate=pl.CostEstimate(flops=1 << 20, bytes_accessed=6 << 20, transcendentals=0),
    )(core, mine, theirs)


def cell_mask(channels):
    cell = lax.broadcasted_iota(jnp.int32, (16, channels * 16), 0)
    col = lax.broadcasted_iota(jnp.int32, (16, channels * 16), 1)
    return cell == col % 16


def spread(channels):
    chan = lax.broadcasted_iota(jnp.int32, (channels, channels * 16), 0)
    col = lax.broadcasted_iota(jnp.int32, (channels, channels * 16), 1)
    return (chan == col // 16).astype(BF)


def stem_matrix(stem_weight):
    channels = stem_weight.shape[0]
    taps = stem_weight.reshape(channels, 36)
    wide = dot(taps, spread(channels), ((0,), (0,))).astype(BF)
    stack = jnp.where(cell_mask(channels)[:, None, :], wide[None], BF(0))
    return dot(jnp.asarray(placement(), BF), stack.reshape(16 * 36, channels * 16)).astype(BF)


def slots_of(route, experts, capacity):
    tokens = route.shape[0]
    hot = (route[:, None] == jnp.arange(experts, dtype=jnp.int32)[None, :]).astype(F32)
    row = lax.broadcasted_iota(jnp.int32, (tokens, tokens), 0)
    col = lax.broadcasted_iota(jnp.int32, (tokens, tokens), 1)
    before = dot((col < row).astype(BF), hot.astype(BF))
    return route * capacity + jnp.sum(before * hot, axis=1).astype(jnp.int32)


def swap(block):
    count = lax.axis_size("core")
    return lax.ppermute(block, "core", [(i, count - 1 - i) for i in range(count)])


def total_over_all(own, other, beside):
    chip = (own + swap(other).astype(F32)).astype(BF)
    parts = lax.all_to_all(chip, HALF, split_axis=0, concat_axis=0, tiled=True)
    parts, done = lax.optimization_barrier((parts, beside(chip)))
    total = jnp.sum(parts.astype(F32), axis=0).astype(BF)
    copies = jnp.broadcast_to(total[None], parts.shape)
    mine = lax.all_to_all(copies, HALF, split_axis=0, concat_axis=0, tiled=True)
    theirs = swap(mine)
    return mine, theirs, done


def to_owners(rows, members):
    copies = jnp.broadcast_to(rows[None], (members, *rows.shape))
    blocks = copies.reshape(lax.axis_size(ALL), -1, rows.shape[1])
    moved = lax.all_to_all(blocks, ALL, split_axis=0, concat_axis=0, tiled=True)
    return moved.reshape(-1, rows.shape[1])


def local(
    raw_tiles,
    stem_weight,
    embed_weight,
    norm_gain,
    router_weight,
    w_gate,
    w_up,
    w_down,
    routes,
    cotangent,
):
    tokens, width = cotangent.shape
    owners = lax.axis_size(DE)
    members = lax.axis_size("tp")
    devices = owners * members
    experts = owners
    capacity = 2 * tokens // experts
    slots = experts * capacity
    w_gate, w_up, w_down = w_gate[0], w_up[0], w_down[0]

    slot_of = slots_of(routes[:, 0], experts, capacity)
    selector = (slot_of[None, :] == jnp.arange(slots, dtype=jnp.int32)[:, None]).astype(BF)
    windows = window_rows(halo_rows(raw_tiles), tokens)
    windows = jnp.pad(windows, ((0, 0), (0, -PIX % 128)))
    sent = dot(selector, jnp.concatenate([cotangent, windows], axis=1)).astype(BF)
    moved = to_owners(lax.optimization_barrier(sent), members)

    conv = jnp.pad(stem_matrix(stem_weight), ((0, -PIX % 128), (0, 0)))
    expert = lax.axis_index(DE)
    router_row = lax.dynamic_slice_in_dim(router_weight, expert, 1, axis=1).reshape(1, width)
    router_row = router_row.astype(F32)
    gain = norm_gain.reshape(1, width)
    core = lax.axis_index("core").reshape(1)
    out_part, hidden, hidden_act, gate_cot, up_cot, out_cot, own, other = layer(
        jnp.concatenate([expert.reshape(1), core]),
        gain, router_row, moved, conv, embed_weight, w_gate, w_up, w_down,
    )
    out_share = lax.psum_scatter(out_part, "tp", scatter_dimension=0, tiled=True)
    mixed = out_share.reshape(experts, capacity, width)
    returned = lax.all_to_all(mixed, DE, split_axis=0, concat_axis=0, tiled=True)
    expert_mix = dot(selector, returned.reshape(slots, width), ((0,), (0,))).astype(BF)

    def weight_grads(ready):
        rows, gates, ups, acts, outs, _ = lax.optimization_barrier(
            (hidden, gate_cot, up_cot, hidden_act, out_cot, ready)
        )
        return (
            dot(rows, gates, ((0,), (0,))),
            dot(rows, ups, ((0,), (0,))),
            dot(acts, outs, ((0,), (0,))),
        )

    mine, theirs, grads = total_over_all(own, other, weight_grads)
    embed_total, router_total, gain_total, stem_total = finish(
        core, mine, theirs, embed_weight.shape[0], width, experts
    )
    stem_total = stem_total[:36, : stem_weight.shape[0]].T
    return (
        expert_mix,
        grads[0][None],
        grads[1][None],
        grads[2][None],
        router_total,
        gain_total.reshape(width),
        embed_total,
        stem_total.reshape(stem_weight.shape),
    )


def solution(mesh):
    owners, members = mesh.devices.shape
    fine = jax.sharding.Mesh(mesh.devices.reshape(owners // 2, 2, members), ("xz", "core", "tp"))
    return jax.shard_map(
        local,
        mesh=fine,
        in_specs=(
            P(None, DE_TP, None),
            P(),
            P(),
            P(),
            P(),
            P(DE, None, "tp"),
            P(DE, None, "tp"),
            P(DE, "tp", None),
            P(DE_TP, None),
            P(DE_TP, None),
        ),
        out_specs=(
            P(DE_TP, None),
            P(DE, None, "tp"),
            P(DE, None, "tp"),
            P(DE, "tp", None),
            P(),
            P(),
            P(),
            P(),
        ),
        check_vma=False,
    )
```

```python
import functools

import jax
import jax.numpy as jnp
import numpy as np
from jax import lax
from jax.experimental import pallas as pl
from jax.experimental.pallas import tpu as pltpu
from jax.sharding import PartitionSpec as P

PATCH = 4
GELU_C = 0.7978845608028654
GELU_A = 0.044715
EPSILON = 1e-06
BF = jnp.bfloat16
F32 = jnp.float32
PIX = 144
DE = ("xz", "core")
DE_TP = ("xz", "core", "tp")
HALF = ("xz", "tp")


def dot(a, b, dims=((1,), (0,))):
    return lax.dot_general(a, b, (dims, ((), ())), preferred_element_type=F32)


def halo_rows(raw):
    count = lax.axis_size(DE_TP)
    forward = [(i, i + 1) for i in range(count - 1)]
    backward = [(target, source) for source, target in forward]
    low = lax.ppermute(raw[:, -1:], DE_TP, forward)
    high = lax.ppermute(raw[:, :1], DE_TP, backward)
    return jnp.concatenate([low, raw, high], axis=1)


def window_rows(padded, tokens):
    chans, rows, cols = padded.shape
    flat = padded.reshape(chans * rows, cols)
    step = lax.broadcasted_iota(jnp.int32, (6, tokens, cols), 0)
    token = lax.broadcasted_iota(jnp.int32, (6, tokens, cols), 1)
    col = lax.broadcasted_iota(jnp.int32, (6, tokens, cols), 2)
    pick = (col == PATCH * token + step - 1).astype(BF)
    out = lax.dot_general(pick, flat, (((2,), (1,)), ((), ())), preferred_element_type=F32)
    return out.transpose(1, 0, 2).reshape(tokens, 6 * chans * rows).astype(BF)


def placement():
    place = np.zeros((6, 4, 6, 16, 4, 3, 3), np.float32)
    for r in range(4):
        for c in range(4):
            for a in range(3):
                for b in range(3):
                    for i in range(4):
                        place[c + b, i, r + a, r * 4 + c, i, a, b] = 1
    return place.reshape(PIX, 16 * 36)


TAPS = 40


def placement_rows():
    place = placement().T.reshape(16, 4, 9, PIX).transpose(0, 2, 1, 3).reshape(16, 36, PIX)
    return np.pad(place, ((0, 0), (0, TAPS - 36), (0, 0))).reshape(16 * TAPS, PIX)


VMEM = pl.BlockSpec(memory_space=pltpu.VMEM)
SMEM = pl.BlockSpec(memory_space=pltpu.SMEM)
HBM = pl.BlockSpec(memory_space=pl.ANY)
ROWS = 256
TALL, LANES = 48, 128


def folded(row):
    return jnp.concatenate([row[:, k : k + LANES] for k in range(0, row.shape[1], LANES)], axis=0)


def layer_kernel(first_group, parts, place_at_ref, gain_ref, router_ref, *refs):
    last = first_group > 0
    cells_hbm, cots_hbm, refs = refs[: parts[0]], refs[parts[0] : sum(parts)], refs[sum(parts) :]
    conv_hbm, embed_hbm, gate_hbm, up_hbm, down_hbm, place_hbm = refs[:6]
    refs = refs[6:]
    if last:
        saved_hbm, saved_sums_ref = refs[6:9], refs[9]
        refs = refs[10:]
    out_hbm, hidden_hbm, act_hbm, gate_cot_hbm, up_cot_hbm, out_cot_hbm = refs[:6]
    if last:
        own_ref, other_ref = refs[6:8]
        refs = refs[8:]
    else:
        save_hbm, sums_ref = refs[6:9], refs[9]
        refs = refs[10:]
    (cells_ref, conv_ref, embed_ref, gate_ref, up_ref, down_ref, cots_ref, place_ref,
     out_ref, hidden_ref, act_ref, gate_cot_ref, up_cot_ref, out_cot_ref, patches_ref, embed_cot_ref, preact_cot_ref,
     in_sems, out_sems) = refs
    total, width = embed_cot_ref.shape
    pixels = patches_ref.shape[1]
    across = width // LANES
    arriving = {}

    def fetch(sources, target, k, first=0):
        copies = []
        for source in sources:
            place = target.at[pl.ds(first, source.shape[0])]
            copies.append(pltpu.make_async_copy(source, place, in_sems.at[k + len(copies)]))
            copies[-1].start()
            first += source.shape[0]
        return copies

    cells_copies = fetch(cells_hbm, cells_ref, 9)
    for k, (name, source, target) in enumerate(
        (
            ("conv", conv_hbm, conv_ref),
            ("embed", embed_hbm, embed_ref),
            ("gate", gate_hbm, gate_ref),
            ("up", up_hbm, up_ref),
            ("down", down_hbm, down_ref),
            ("place", place_hbm, place_ref),
        )
    ):
        if last or name != "place":
            arriving[name] = pltpu.make_async_copy(source, target, in_sems.at[k])
            arriving[name].start()
    cots_copies = fetch(cots_hbm, cots_ref, 9 + len(cells_copies))
    if last:
        for k, (source, target) in enumerate(zip(saved_hbm, (patches_ref, embed_cot_ref, preact_cot_ref))):
            place = target.at[pl.ds(0, source.shape[0])]
            arriving[k] = pltpu.make_async_copy(source, place, in_sems.at[6 + k])
            arriving[k].start()

    def need(name):
        if name in arriving:
            arriving.pop(name).wait()

    leaving = []

    def send(rows, k, source, target, place=None):
        group = rows.start // ROWS
        if place is None:
            place = pl.ds((first_group + group) * ROWS, ROWS)
        leaving.append(pltpu.make_async_copy(source.at[rows], target.at[place], out_sems.at[group, k]))
        leaving[-1].start()

    router_sum = saved_sums_ref[0:1] if last else jnp.zeros((1, width), F32)
    gain_sum = saved_sums_ref[1:2] if last else jnp.zeros((1, width), F32)
    for first in range(0, cots_ref.shape[0], ROWS):
        rows = slice(first, first + ROWS)
        kept = slice(first_group * ROWS + first, first_group * ROWS + first + ROWS)
        for copy in cells_copies:
            copy.wait()
        cells_copies = []
        need("conv")
        preact = dot(cells_ref[kept], conv_ref[...])
        square = preact * preact
        tanh_v = jnp.tanh(GELU_C * (preact + GELU_A * square * preact))
        half = 0.5 * (1.0 + tanh_v)
        patches = (preact * half).astype(BF)
        patches_ref[kept] = patches
        slope = half + 0.5 * preact * (1.0 - tanh_v * tanh_v) * GELU_C * (1.0 + 3.0 * GELU_A * square)
        need("embed")
        embedded = dot(patches, embed_ref[...])
        inv_rms = lax.rsqrt(jnp.mean(embedded * embedded, axis=-1, keepdims=True) + EPSILON)
        normed = embedded * inv_rms
        hidden = (normed * gain_ref[...]).astype(BF)
        hidden_ref[rows] = hidden
        send(rows, 0, hidden_ref, hidden_hbm)
        logit = jnp.sum(hidden.astype(F32) * router_ref[...], axis=1, keepdims=True)
        score = jax.nn.sigmoid(logit)
        need("gate")
        gate_proj = dot(hidden, gate_ref[...])
        need("up")
        up_proj = dot(hidden, up_ref[...])
        sigmoid_gate = jax.nn.sigmoid(gate_proj)
        activated = gate_proj * sigmoid_gate
        factor = up_proj * (sigmoid_gate + activated * (1.0 - sigmoid_gate))
        hidden_act = (activated * up_proj).astype(BF)
        act_ref[rows] = hidden_act
        send(rows, 1, act_ref, act_hbm)
        need("down")
        out_ref[rows] = (score * dot(hidden_act, down_ref[...])).astype(BF)
        place = place_at_ref[2 + first_group + first // ROWS] * ROWS
        send(rows, 2, out_ref, out_hbm, pl.ds(pl.multiple_of(place, ROWS), ROWS))
        for copy in cots_copies:
            copy.wait()
        cots_copies = []
        cot = cots_ref[rows]
        act_raw = dot(cot, down_ref[...], ((1,), (1,)))
        score_grad = jnp.sum(hidden_act.astype(F32) * act_raw, axis=1, keepdims=True)
        logit_cot = score_grad * score * (1.0 - score)
        out_cot_ref[rows] = (score * cot.astype(F32)).astype(BF)
        send(rows, 3, out_cot_ref, out_cot_hbm)
        act_cot = score * act_raw
        gate_cot = (act_cot * factor).astype(BF)
        up_cot = (act_cot * activated).astype(BF)
        gate_cot_ref[rows] = gate_cot
        send(rows, 4, gate_cot_ref, gate_cot_hbm)
        up_cot_ref[rows] = up_cot
        send(rows, 5, up_cot_ref, up_cot_hbm)
        slot_cot = dot(gate_cot, gate_ref[...], ((1,), (1,))) + dot(up_cot, up_ref[...], ((1,), (1,)))
        upstream = slot_cot + logit_cot * router_ref[...]
        scaled = upstream * gain_ref[...]
        mean = jnp.mean(scaled * normed, axis=-1, keepdims=True)
        embed_cot = (inv_rms * (scaled - normed * mean)).astype(BF)
        embed_cot_ref[kept] = embed_cot
        router_sum += jnp.sum(hidden.astype(F32) * logit_cot, axis=0, keepdims=True)
        gain_sum += jnp.sum(upstream * normed, axis=0, keepdims=True)
        feature_cot = dot(embed_cot, embed_ref[...], ((1,), (1,)))
        preact_cot_ref[kept] = (feature_cot * slope).astype(BF)

    if not last:
        sums_ref[...] = jnp.concatenate([router_sum, gain_sum, jnp.zeros((6, width), F32)], axis=0)
        for k, (source, target) in enumerate(zip((patches_ref, embed_cot_ref, preact_cot_ref), save_hbm)):
            leaving.append(pltpu.make_async_copy(source, target, out_sems.at[0, 6 + k]))
            leaving[-1].start()
        for copy in leaving:
            copy.wait()
        return

    for k in range(3):
        need(k)
    product_sum = dot(cells_ref[...], preact_cot_ref[...], ((0,), (0,)))
    need("place")
    taps = dot(place_ref[...], product_sum.astype(BF))
    col = lax.broadcasted_iota(jnp.int32, (TAPS, pixels), 1)
    wide = jnp.zeros((TAPS, pixels), F32)
    for cell in range(16):
        wide += jnp.where(col % 16 == cell, taps[cell * TAPS : cell * TAPS + TAPS], 0.0)
    chan = lax.broadcasted_iota(jnp.int32, (LANES, pixels), 0)
    group = lax.broadcasted_iota(jnp.int32, (LANES, pixels), 1)
    stem = dot(wide.astype(BF), (chan == group // 16).astype(BF), ((1,), (1,)))
    router = folded(router_sum)
    gain = folded(gain_sum)
    expert, core = place_at_ref[0], place_at_ref[1]

    def small(p):
        if p < 32:
            return jnp.where(expert == p, router, 0.0)
        if p == 32:
            return gain
        if p < 38:
            return stem[8 * (p - 33) : 8 * (p - 33) + 8]
        return jnp.zeros((8, LANES), F32)

    part = pixels // 2
    for target, side in ((other_ref, 1 - core), (own_ref, core)):
        columns = pl.ds(pl.multiple_of(side * part, LANES), part)
        embed_part = dot(patches_ref[:, columns], embed_cot_ref[...], ((0,), (0,)))
        for a in range(part // TALL):
            for b in range(across):
                p = a * across + b
                main = embed_part[a * TALL : a * TALL + TALL, b * LANES : b * LANES + LANES]
                rest = jnp.where(side == 0, small(p), 0.0)
                target[p] = jnp.concatenate([main, rest], axis=0).astype(target.dtype)
    for copy in leaving:
        copy.wait()


def layer(first_group, groups, place_at, gain, router_row, cells, cots, weights, saved):
    conv, embed_weight, w_gate, w_up, w_down = weights
    width = gain.shape[1]
    units = w_gate.shape[1]
    pixels = conv.shape[1]
    extra = cells[0].shape[1]
    rows = sum(array.shape[0] for array in cots)
    kept = first_group * ROWS + rows
    place = jnp.asarray(placement_rows(), BF)
    place = jnp.pad(place, ((0, 0), (0, extra - PIX)))
    ins = (place_at, gain, router_row, *cells, *cots, *weights, place)
    outs = (width, width, units, units, units, width)
    keeps = (pixels, width, pixels)
    shapes = [jax.ShapeDtypeStruct((groups * ROWS, size), BF) for size in outs]
    if saved:
        shapes += [
            jax.ShapeDtypeStruct((64, TALL + 8, LANES), F32),
            jax.ShapeDtypeStruct((64, TALL + 8, LANES), BF),
        ]
        out_specs = [HBM] * len(outs) + [VMEM] * 2
    else:
        shapes += [jax.ShapeDtypeStruct((rows, size), BF) for size in keeps] + [jax.ShapeDtypeStruct((8, width), F32)]
        out_specs = [HBM] * (len(outs) + 3) + [VMEM]
    return pl.pallas_call(
        functools.partial(layer_kernel, first_group, (len(cells), len(cots))),
        in_specs=[SMEM, VMEM, VMEM] + [HBM] * (len(ins) - 3) + ([HBM] * 9 + [VMEM] if saved else []),
        out_specs=out_specs,
        out_shape=shapes,
        input_output_aliases={len(ins) + k: k for k in range(6)} if saved else {},
        scratch_shapes=[
            pltpu.VMEM((kept, extra), BF),
            pltpu.VMEM(conv.shape, BF),
            pltpu.VMEM(embed_weight.shape, BF),
            pltpu.VMEM(w_gate.shape, BF),
            pltpu.VMEM(w_up.shape, BF),
            pltpu.VMEM(w_down.shape, BF),
            pltpu.VMEM((rows, width), BF),
            pltpu.VMEM(place.shape, BF),
        ]
        + [pltpu.VMEM((rows, size), BF) for size in outs]
        + [pltpu.VMEM((kept, size), BF) for size in keeps]
        + [
            pltpu.SemaphoreType.DMA((9 + len(cells) + len(cots),)),
            pltpu.SemaphoreType.DMA((rows // ROWS, 9)),
        ],
        compiler_params=pltpu.CompilerParams(vmem_limit_bytes=56 << 20),
        cost_estimate=pl.CostEstimate(
            flops=rows // ROWS * (4 << 30), bytes_accessed=(8 << 20) + rows // ROWS * (5 << 20), transcendentals=0
        ),
    )(*ins, *saved)


def finish_kernel(core_ref, mine_ref, theirs_ref, embed_ref, router_ref, gain_ref, stem_ref):
    first = core_ref[0] == 0
    count = mine_ref.shape[0]
    tall, lanes = 48, 128
    across = embed_ref.shape[1] // lanes

    def piece(p):
        near = mine_ref[p % count].astype(F32)
        far = theirs_ref[p % count].astype(F32)
        return jnp.where(first, near, far) if p < count else jnp.where(first, far, near)

    experts = router_ref.shape[0]
    rows = []
    for p in range(2 * count):
        value = piece(p)
        a, b = p // across, p % across
        embed_ref[a * tall : a * tall + tall, b * lanes : b * lanes + lanes] = value[:tall]
        if p < experts:
            rows.append(value[tall:])
        elif p == experts:
            gain_ref[...] = value[tall:]
        elif p < experts + 6:
            k = p - experts - 1
            stem_ref[8 * k : 8 * k + 8, :] = value[tall:]
    for k in range(across):
        block = jnp.concatenate([row[k : k + 1] for row in rows], axis=0)
        router_ref[:, k * lanes : k * lanes + lanes] = block


def finish(core, mine, theirs, pixels, width, experts):
    return pl.pallas_call(
        finish_kernel,
        in_specs=[
            pl.BlockSpec(memory_space=pltpu.SMEM),
            pl.BlockSpec(memory_space=pltpu.VMEM),
            pl.BlockSpec(memory_space=pltpu.VMEM),
        ],
        out_specs=[pl.BlockSpec(memory_space=pltpu.VMEM)] * 4,
        out_shape=[
            jax.ShapeDtypeStruct((pixels, width), F32),
            jax.ShapeDtypeStruct((experts, width), F32),
            jax.ShapeDtypeStruct((8, 128), F32),
            jax.ShapeDtypeStruct((TAPS, 128), F32),
        ],
        compiler_params=pltpu.CompilerParams(vmem_limit_bytes=32 << 20),
        cost_estimate=pl.CostEstimate(flops=1 << 20, bytes_accessed=6 << 20, transcendentals=0),
    )(core, mine, theirs)


def cell_mask(channels):
    cell = lax.broadcasted_iota(jnp.int32, (16, channels * 16), 0)
    col = lax.broadcasted_iota(jnp.int32, (16, channels * 16), 1)
    return cell == col % 16


def spread(channels):
    chan = lax.broadcasted_iota(jnp.int32, (channels, channels * 16), 0)
    col = lax.broadcasted_iota(jnp.int32, (channels, channels * 16), 1)
    return (chan == col // 16).astype(BF)


def stem_matrix(stem_weight):
    channels = stem_weight.shape[0]
    taps = stem_weight.reshape(channels, 36)
    wide = dot(taps, spread(channels), ((0,), (0,))).astype(BF)
    stack = jnp.where(cell_mask(channels)[:, None, :], wide[None], BF(0))
    return dot(jnp.asarray(placement(), BF), stack.reshape(16 * 36, channels * 16)).astype(BF)


def slots_of(route, experts, capacity):
    tokens = route.shape[0]
    hot = (route[:, None] == jnp.arange(experts, dtype=jnp.int32)[None, :]).astype(F32)
    row = lax.broadcasted_iota(jnp.int32, (tokens, tokens), 0)
    col = lax.broadcasted_iota(jnp.int32, (tokens, tokens), 1)
    before = dot((col < row).astype(BF), hot.astype(BF))
    return route * capacity + jnp.sum(before * hot, axis=1).astype(jnp.int32)


def swap(block):
    count = lax.axis_size("core")
    return lax.ppermute(block, "core", [(i, count - 1 - i) for i in range(count)])


def total_over_all(own, other, beside):
    chip = (own + swap(other).astype(F32)).astype(BF)
    parts = lax.all_to_all(chip, HALF, split_axis=0, concat_axis=0, tiled=True)
    parts, done = lax.optimization_barrier((parts, beside(chip)))
    total = jnp.sum(parts.astype(F32), axis=0).astype(BF)
    copies = jnp.broadcast_to(total[None], parts.shape)
    mine = lax.all_to_all(copies, HALF, split_axis=0, concat_axis=0, tiled=True)
    theirs = swap(mine)
    return mine, theirs, done


def shifted(block, step):
    count = lax.axis_size("tp")
    return lax.ppermute(block, "tp", [(i, (i + step) % count) for i in range(count)])


def local(
    raw_tiles,
    stem_weight,
    embed_weight,
    norm_gain,
    router_weight,
    w_gate,
    w_up,
    w_down,
    routes,
    cotangent,
):
    tokens, width = cotangent.shape
    owners = lax.axis_size(DE)
    members = lax.axis_size("tp")
    experts = owners
    capacity = 2 * tokens // experts
    slots = experts * capacity
    w_gate, w_up, w_down = w_gate[0], w_up[0], w_down[0]

    slot_of = slots_of(routes[:, 0], experts, capacity)
    selector = (slot_of[None, :] == jnp.arange(slots, dtype=jnp.int32)[:, None]).astype(BF)
    sent_cots = dot(selector, cotangent).astype(BF).reshape(experts, capacity, width)
    sent_cots, raw_tiles = lax.optimization_barrier((sent_cots, raw_tiles))
    own_cots = lax.all_to_all(sent_cots, DE, split_axis=0, concat_axis=0, tiled=True).reshape(slots, width)
    before, after = shifted(own_cots, 1), shifted(own_cots, -1)
    windows = window_rows(halo_rows(raw_tiles), tokens)
    windows = jnp.pad(windows, ((0, 0), (0, -PIX % 128)))
    windows = dot(selector, windows).astype(BF).reshape(experts, capacity, -1)
    windows, _ = lax.optimization_barrier((windows, own_cots))
    own_cells = lax.all_to_all(windows, DE, split_axis=0, concat_axis=0, tiled=True).reshape(slots, -1)
    middle = slots // 2
    cots = [own_cots, before, after, shifted(before[:middle], 1), shifted(after[middle:], -1)]
    cells = [own_cells, shifted(own_cells, 1), shifted(own_cells, -1), shifted(own_cells, 2)]
    member = lax.axis_index("tp")
    sources = jnp.remainder(member + jnp.array([0, -1, 1, 2], jnp.int32), members)

    conv = jnp.pad(stem_matrix(stem_weight), ((0, -PIX % 128), (0, 0)))
    expert = lax.axis_index(DE)
    router_row = lax.dynamic_slice_in_dim(router_weight, expert, 1, axis=1).reshape(1, width)
    router_row = router_row.astype(F32)
    gain = norm_gain.reshape(1, width)
    core = lax.axis_index("core").reshape(1)
    place_at = jnp.concatenate([expert.reshape(1), core, sources])
    weights = (conv, embed_weight, w_gate, w_up, w_down)
    saved = layer(0, members, place_at, gain, router_row, cells[:1], cots[:1], weights, ())
    out_part, hidden, hidden_act, gate_cot, up_cot, out_cot, own, other = layer(
        1, members, place_at, gain, router_row, cells, cots[1:], weights, saved
    )
    out_share = lax.psum_scatter(out_part, "tp", scatter_dimension=0, tiled=True)
    mixed = out_share.reshape(experts, capacity, width)
    returned = lax.all_to_all(mixed, DE, split_axis=0, concat_axis=0, tiled=True)
    expert_mix = dot(selector, returned.reshape(slots, width), ((0,), (0,))).astype(BF)

    def weight_grads(ready):
        rows, gates, ups, acts, outs, _ = lax.optimization_barrier(
            (hidden, gate_cot, up_cot, hidden_act, out_cot, ready)
        )
        return (
            dot(rows, gates, ((0,), (0,))),
            dot(rows, ups, ((0,), (0,))),
            dot(acts, outs, ((0,), (0,))),
        )

    mine, theirs, grads = total_over_all(own, other, weight_grads)
    embed_total, router_total, gain_total, stem_total = finish(
        core, mine, theirs, embed_weight.shape[0], width, experts
    )
    stem_total = stem_total[:36, : stem_weight.shape[0]].reshape(3, 3, 4, -1).transpose(3, 2, 0, 1)
    return (
        expert_mix,
        grads[0][None],
        grads[1][None],
        grads[2][None],
        router_total.T,
        gain_total.reshape(width),
        embed_total,
        stem_total,
    )


def solution(mesh):
    owners, members = mesh.devices.shape
    fine = jax.sharding.Mesh(mesh.devices.reshape(owners // 2, 2, members), ("xz", "core", "tp"))
    return jax.shard_map(
        local,
        mesh=fine,
        in_specs=(
            P(None, DE_TP, None),
            P(),
            P(),
            P(),
            P(),
            P(DE, None, "tp"),
            P(DE, None, "tp"),
            P(DE, "tp", None),
            P(DE_TP, None),
            P(DE_TP, None),
        ),
        out_specs=(
            P(DE_TP, None),
            P(DE, None, "tp"),
            P(DE, None, "tp"),
            P(DE, "tp", None),
            P(),
            P(),
            P(),
            P(),
        ),
        check_vma=False,
    )
```

```python
import functools

import jax
import jax.numpy as jnp
import numpy as np
from jax import lax
from jax.experimental import pallas as pl
from jax.experimental.pallas import tpu as pltpu
from jax.sharding import PartitionSpec as P

PATCH = 4
GELU_C = 0.7978845608028654
GELU_A = 0.044715
EPSILON = 1e-06
BF = jnp.bfloat16
F32 = jnp.float32
PIX = 144
DE = ("xz", "core")
DE_TP = ("xz", "core", "tp")
HALF = ("xz", "tp")


def dot(a, b, dims=((1,), (0,))):
    return lax.dot_general(a, b, (dims, ((), ())), preferred_element_type=F32)


def halo_rows(raw):
    count = lax.axis_size(DE_TP)
    forward = [(i, i + 1) for i in range(count - 1)]
    backward = [(target, source) for source, target in forward]
    low = lax.ppermute(raw[:, -1:], DE_TP, forward)
    high = lax.ppermute(raw[:, :1], DE_TP, backward)
    return jnp.concatenate([low, raw, high], axis=1)


def window_rows(padded, tokens):
    chans, rows, cols = padded.shape
    flat = padded.reshape(chans * rows, cols)
    step = lax.broadcasted_iota(jnp.int32, (6, tokens, cols), 0)
    token = lax.broadcasted_iota(jnp.int32, (6, tokens, cols), 1)
    col = lax.broadcasted_iota(jnp.int32, (6, tokens, cols), 2)
    pick = (col == PATCH * token + step - 1).astype(BF)
    out = lax.dot_general(pick, flat, (((2,), (1,)), ((), ())), preferred_element_type=F32)
    return out.transpose(1, 0, 2).reshape(tokens, 6 * chans * rows).astype(BF)


def placement():
    place = np.zeros((6, 4, 6, 16, 4, 3, 3), np.float32)
    for r in range(4):
        for c in range(4):
            for a in range(3):
                for b in range(3):
                    for i in range(4):
                        place[c + b, i, r + a, r * 4 + c, i, a, b] = 1
    return place.reshape(PIX, 16 * 36)


TAPS = 40


def placement_rows():
    place = placement().T.reshape(16, 4, 9, PIX).transpose(0, 2, 1, 3).reshape(16, 36, PIX)
    return np.pad(place, ((0, 0), (0, TAPS - 36), (0, 0))).reshape(16 * TAPS, PIX)


VMEM = pl.BlockSpec(memory_space=pltpu.VMEM)
SMEM = pl.BlockSpec(memory_space=pltpu.SMEM)
HBM = pl.BlockSpec(memory_space=pl.ANY)
ROWS = 256
TALL, LANES = 48, 128


def folded(row):
    return jnp.concatenate([row[:, k : k + LANES] for k in range(0, row.shape[1], LANES)], axis=0)


def layer_kernel(first_group, parts, place_at_ref, gain_ref, router_ref, *refs):
    last = first_group > 0
    cells_hbm, cots_hbm, refs = refs[: parts[0]], refs[parts[0] : sum(parts)], refs[sum(parts) :]
    conv_hbm, embed_hbm, gate_hbm, up_hbm, down_hbm, place_hbm = refs[:6]
    refs = refs[6:]
    if last:
        saved_hbm, saved_sums_ref = refs[6:9], refs[9]
        refs = refs[10:]
    out_hbm, hidden_hbm, act_hbm, gate_cot_hbm, up_cot_hbm, out_cot_hbm = refs[:6]
    if last:
        own_ref, other_ref = refs[6:8]
        refs = refs[8:]
    else:
        save_hbm, sums_ref = refs[6:9], refs[9]
        refs = refs[10:]
    (cells_ref, conv_ref, embed_ref, gate_ref, up_ref, down_ref, cots_ref, place_ref,
     out_ref, hidden_ref, act_ref, gate_cot_ref, up_cot_ref, out_cot_ref, patches_ref, embed_cot_ref, preact_cot_ref,
     in_sems, out_sems) = refs
    total, width = embed_cot_ref.shape
    pixels = patches_ref.shape[1]
    across = width // LANES
    arriving = {}

    def fetch(sources, target, k, first=0):
        copies = []
        for source in sources:
            place = target.at[pl.ds(first, source.shape[0])]
            copies.append(pltpu.make_async_copy(source, place, in_sems.at[k + len(copies)]))
            copies[-1].start()
            first += source.shape[0]
        return copies

    cells_copies = fetch(cells_hbm, cells_ref, 9)
    for k, (name, source, target) in enumerate(
        (
            ("conv", conv_hbm, conv_ref),
            ("embed", embed_hbm, embed_ref),
            ("gate", gate_hbm, gate_ref),
            ("up", up_hbm, up_ref),
            ("down", down_hbm, down_ref),
            ("place", place_hbm, place_ref),
        )
    ):
        if last or name != "place":
            arriving[name] = pltpu.make_async_copy(source, target, in_sems.at[k])
            arriving[name].start()
    cots_copies = fetch(cots_hbm, cots_ref, 9 + len(cells_copies))
    if last:
        for k, (source, target) in enumerate(zip(saved_hbm, (patches_ref, embed_cot_ref, preact_cot_ref))):
            place = target.at[pl.ds(0, source.shape[0])]
            arriving[k] = pltpu.make_async_copy(source, place, in_sems.at[6 + k])
            arriving[k].start()

    def need(name):
        if name in arriving:
            arriving.pop(name).wait()

    leaving = []

    def send(rows, k, source, target, place=None):
        group = rows.start // ROWS
        if place is None:
            place = pl.ds((first_group + group) * ROWS, ROWS)
        leaving.append(pltpu.make_async_copy(source.at[rows], target.at[place], out_sems.at[group, k]))
        leaving[-1].start()

    router_sum = saved_sums_ref[0:1] if last else jnp.zeros((1, width), F32)
    gain_sum = saved_sums_ref[1:2] if last else jnp.zeros((1, width), F32)
    for first in range(0, cots_ref.shape[0], ROWS):
        rows = slice(first, first + ROWS)
        kept = slice(first_group * ROWS + first, first_group * ROWS + first + ROWS)
        for copy in cells_copies:
            copy.wait()
        cells_copies = []
        need("conv")
        preact = dot(cells_ref[kept], conv_ref[...])
        square = preact * preact
        tanh_v = jnp.tanh(GELU_C * (preact + GELU_A * square * preact))
        half = 0.5 * (1.0 + tanh_v)
        patches = (preact * half).astype(BF)
        patches_ref[kept] = patches
        slope = half + 0.5 * preact * (1.0 - tanh_v * tanh_v) * GELU_C * (1.0 + 3.0 * GELU_A * square)
        need("embed")
        embedded = dot(patches, embed_ref[...])
        inv_rms = lax.rsqrt(jnp.mean(embedded * embedded, axis=-1, keepdims=True) + EPSILON)
        normed = embedded * inv_rms
        hidden = (normed * gain_ref[...]).astype(BF)
        hidden_ref[rows] = hidden
        send(rows, 0, hidden_ref, hidden_hbm)
        logit = jnp.sum(hidden.astype(F32) * router_ref[...], axis=1, keepdims=True)
        score = jax.nn.sigmoid(logit)
        need("gate")
        gate_proj = dot(hidden, gate_ref[...])
        need("up")
        up_proj = dot(hidden, up_ref[...])
        sigmoid_gate = jax.nn.sigmoid(gate_proj)
        activated = gate_proj * sigmoid_gate
        factor = up_proj * (sigmoid_gate + activated * (1.0 - sigmoid_gate))
        hidden_act = (activated * up_proj).astype(BF)
        act_ref[rows] = hidden_act
        send(rows, 1, act_ref, act_hbm)
        need("down")
        out_ref[rows] = (score * dot(hidden_act, down_ref[...])).astype(BF)
        place = place_at_ref[2 + first_group + first // ROWS] * ROWS
        send(rows, 2, out_ref, out_hbm, pl.ds(pl.multiple_of(place, ROWS), ROWS))
        for copy in cots_copies:
            copy.wait()
        cots_copies = []
        cot = cots_ref[rows]
        act_raw = dot(cot, down_ref[...], ((1,), (1,)))
        score_grad = jnp.sum(hidden_act.astype(F32) * act_raw, axis=1, keepdims=True)
        logit_cot = score_grad * score * (1.0 - score)
        out_cot_ref[rows] = (score * cot.astype(F32)).astype(BF)
        send(rows, 3, out_cot_ref, out_cot_hbm)
        act_cot = score * act_raw
        gate_cot = (act_cot * factor).astype(BF)
        up_cot = (act_cot * activated).astype(BF)
        gate_cot_ref[rows] = gate_cot
        send(rows, 4, gate_cot_ref, gate_cot_hbm)
        up_cot_ref[rows] = up_cot
        send(rows, 5, up_cot_ref, up_cot_hbm)
        slot_cot = dot(gate_cot, gate_ref[...], ((1,), (1,))) + dot(up_cot, up_ref[...], ((1,), (1,)))
        upstream = slot_cot + logit_cot * router_ref[...]
        scaled = upstream * gain_ref[...]
        mean = jnp.mean(scaled * normed, axis=-1, keepdims=True)
        embed_cot = (inv_rms * (scaled - normed * mean)).astype(BF)
        embed_cot_ref[kept] = embed_cot
        router_sum += jnp.sum(hidden.astype(F32) * logit_cot, axis=0, keepdims=True)
        gain_sum += jnp.sum(upstream * normed, axis=0, keepdims=True)
        feature_cot = dot(embed_cot, embed_ref[...], ((1,), (1,)))
        preact_cot_ref[kept] = (feature_cot * slope).astype(BF)

    if not last:
        sums_ref[...] = jnp.concatenate([router_sum, gain_sum, jnp.zeros((6, width), F32)], axis=0)
        for k, (source, target) in enumerate(zip((patches_ref, embed_cot_ref, preact_cot_ref), save_hbm)):
            leaving.append(pltpu.make_async_copy(source, target, out_sems.at[0, 6 + k]))
            leaving[-1].start()
        for copy in leaving:
            copy.wait()
        return

    for k in range(3):
        need(k)
    product_sum = dot(cells_ref[...], preact_cot_ref[...], ((0,), (0,)))
    need("place")
    taps = dot(place_ref[...], product_sum.astype(BF))
    col = lax.broadcasted_iota(jnp.int32, (TAPS, pixels), 1)
    wide = jnp.zeros((TAPS, pixels), F32)
    for cell in range(16):
        wide += jnp.where(col % 16 == cell, taps[cell * TAPS : cell * TAPS + TAPS], 0.0)
    chan = lax.broadcasted_iota(jnp.int32, (LANES, pixels), 0)
    group = lax.broadcasted_iota(jnp.int32, (LANES, pixels), 1)
    stem = dot(wide.astype(BF), (chan == group // 16).astype(BF), ((1,), (1,)))
    router = folded(router_sum)
    gain = folded(gain_sum)
    expert, core = place_at_ref[0], place_at_ref[1]

    def small(p):
        if p < 32:
            return jnp.where(expert == p, router, 0.0)
        if p == 32:
            return gain
        if p < 38:
            return stem[8 * (p - 33) : 8 * (p - 33) + 8]
        return jnp.zeros((8, LANES), F32)

    part = pixels // 2
    for target, side in ((other_ref, 1 - core), (own_ref, core)):
        columns = pl.ds(pl.multiple_of(side * part, LANES), part)
        embed_part = dot(patches_ref[:, columns], embed_cot_ref[...], ((0,), (0,)))
        for a in range(part // TALL):
            for b in range(across):
                p = a * across + b
                main = embed_part[a * TALL : a * TALL + TALL, b * LANES : b * LANES + LANES]
                rest = jnp.where(side == 0, small(p), 0.0)
                target[p] = jnp.concatenate([main, rest], axis=0).astype(target.dtype)
    for copy in leaving:
        copy.wait()


def layer(first_group, groups, place_at, gain, router_row, cells, cots, weights, saved):
    conv, embed_weight, w_gate, w_up, w_down = weights
    width = gain.shape[1]
    units = w_gate.shape[1]
    pixels = conv.shape[1]
    extra = cells[0].shape[1]
    rows = sum(array.shape[0] for array in cots)
    kept = first_group * ROWS + rows
    place = jnp.asarray(placement_rows(), BF)
    place = jnp.pad(place, ((0, 0), (0, extra - PIX)))
    ins = (place_at, gain, router_row, *cells, *cots, *weights, place)
    outs = (width, width, units, units, units, width)
    keeps = (pixels, width, pixels)
    shapes = [jax.ShapeDtypeStruct((groups * ROWS, size), BF) for size in outs]
    if saved:
        shapes += [
            jax.ShapeDtypeStruct((64, TALL + 8, LANES), F32),
            jax.ShapeDtypeStruct((64, TALL + 8, LANES), BF),
        ]
        out_specs = [HBM] * len(outs) + [VMEM] * 2
    else:
        shapes += [jax.ShapeDtypeStruct((rows, size), BF) for size in keeps] + [jax.ShapeDtypeStruct((8, width), F32)]
        out_specs = [HBM] * (len(outs) + 3) + [VMEM]
    return pl.pallas_call(
        functools.partial(layer_kernel, first_group, (len(cells), len(cots))),
        in_specs=[SMEM, VMEM, VMEM] + [HBM] * (len(ins) - 3) + ([HBM] * 9 + [VMEM] if saved else []),
        out_specs=out_specs,
        out_shape=shapes,
        input_output_aliases={len(ins) + k: k for k in range(6)} if saved else {},
        scratch_shapes=[
            pltpu.VMEM((kept, extra), BF),
            pltpu.VMEM(conv.shape, BF),
            pltpu.VMEM(embed_weight.shape, BF),
            pltpu.VMEM(w_gate.shape, BF),
            pltpu.VMEM(w_up.shape, BF),
            pltpu.VMEM(w_down.shape, BF),
            pltpu.VMEM((rows, width), BF),
            pltpu.VMEM(place.shape, BF),
        ]
        + [pltpu.VMEM((rows, size), BF) for size in outs]
        + [pltpu.VMEM((kept, size), BF) for size in keeps]
        + [
            pltpu.SemaphoreType.DMA((9 + len(cells) + len(cots),)),
            pltpu.SemaphoreType.DMA((rows // ROWS, 9)),
        ],
        compiler_params=pltpu.CompilerParams(vmem_limit_bytes=56 << 20),
        cost_estimate=pl.CostEstimate(
            flops=rows // ROWS * (4 << 30), bytes_accessed=(8 << 20) + rows // ROWS * (5 << 20), transcendentals=0
        ),
    )(*ins, *saved)


def finish_kernel(core_ref, mine_ref, theirs_ref, embed_ref, router_ref, gain_ref, stem_ref):
    first = core_ref[0] == 0
    count = mine_ref.shape[0]
    tall, lanes = 48, 128
    across = embed_ref.shape[1] // lanes

    def piece(p):
        near = mine_ref[p % count].astype(F32)
        far = theirs_ref[p % count].astype(F32)
        return jnp.where(first, near, far) if p < count else jnp.where(first, far, near)

    experts = router_ref.shape[0]
    rows = []
    for p in range(2 * count):
        value = piece(p)
        a, b = p // across, p % across
        embed_ref[a * tall : a * tall + tall, b * lanes : b * lanes + lanes] = value[:tall]
        if p < experts:
            rows.append(value[tall:])
        elif p == experts:
            gain_ref[...] = value[tall:]
        elif p < experts + 6:
            k = p - experts - 1
            stem_ref[8 * k : 8 * k + 8, :] = value[tall:]
    for k in range(across):
        block = jnp.concatenate([row[k : k + 1] for row in rows], axis=0)
        router_ref[:, k * lanes : k * lanes + lanes] = block


def finish(core, mine, theirs, pixels, width, experts):
    return pl.pallas_call(
        finish_kernel,
        in_specs=[
            pl.BlockSpec(memory_space=pltpu.SMEM),
            pl.BlockSpec(memory_space=pltpu.VMEM),
            pl.BlockSpec(memory_space=pltpu.VMEM),
        ],
        out_specs=[pl.BlockSpec(memory_space=pltpu.VMEM)] * 4,
        out_shape=[
            jax.ShapeDtypeStruct((pixels, width), F32),
            jax.ShapeDtypeStruct((experts, width), F32),
            jax.ShapeDtypeStruct((8, 128), F32),
            jax.ShapeDtypeStruct((TAPS, 128), F32),
        ],
        compiler_params=pltpu.CompilerParams(vmem_limit_bytes=32 << 20),
        cost_estimate=pl.CostEstimate(flops=1 << 20, bytes_accessed=6 << 20, transcendentals=0),
    )(core, mine, theirs)


def cell_mask(channels):
    cell = lax.broadcasted_iota(jnp.int32, (16, channels * 16), 0)
    col = lax.broadcasted_iota(jnp.int32, (16, channels * 16), 1)
    return cell == col % 16


def spread(channels):
    chan = lax.broadcasted_iota(jnp.int32, (channels, channels * 16), 0)
    col = lax.broadcasted_iota(jnp.int32, (channels, channels * 16), 1)
    return (chan == col // 16).astype(BF)


def stem_matrix(stem_weight):
    channels = stem_weight.shape[0]
    taps = stem_weight.reshape(channels, 36)
    wide = dot(taps, spread(channels), ((0,), (0,))).astype(BF)
    stack = jnp.where(cell_mask(channels)[:, None, :], wide[None], BF(0))
    return dot(jnp.asarray(placement(), BF), stack.reshape(16 * 36, channels * 16)).astype(BF)


def slots_of(route, experts, capacity):
    tokens = route.shape[0]
    hot = (route[:, None] == jnp.arange(experts, dtype=jnp.int32)[None, :]).astype(F32)
    row = lax.broadcasted_iota(jnp.int32, (tokens, tokens), 0)
    col = lax.broadcasted_iota(jnp.int32, (tokens, tokens), 1)
    before = dot((col < row).astype(BF), hot.astype(BF))
    return route * capacity + jnp.sum(before * hot, axis=1).astype(jnp.int32)


def swap(block):
    count = lax.axis_size("core")
    return lax.ppermute(block, "core", [(i, count - 1 - i) for i in range(count)])


def total_over_all(own, other, beside):
    chip = (own + swap(other).astype(F32)).astype(BF)
    parts = lax.all_to_all(chip, HALF, split_axis=0, concat_axis=0, tiled=True)
    parts, done = lax.optimization_barrier((parts, beside(chip)))
    total = jnp.sum(parts.astype(F32), axis=0).astype(BF)
    copies = jnp.broadcast_to(total[None], parts.shape)
    mine = lax.all_to_all(copies, HALF, split_axis=0, concat_axis=0, tiled=True)
    theirs = swap(mine)
    return mine, theirs, done


def shifted(block, step):
    count = lax.axis_size("tp")
    return lax.ppermute(block, "tp", [(i, (i + step) % count) for i in range(count)])


def local(
    raw_tiles,
    stem_weight,
    embed_weight,
    norm_gain,
    router_weight,
    w_gate,
    w_up,
    w_down,
    routes,
    cotangent,
):
    tokens, width = cotangent.shape
    owners = lax.axis_size(DE)
    members = lax.axis_size("tp")
    experts = owners
    capacity = 2 * tokens // experts
    slots = experts * capacity
    w_gate, w_up, w_down = w_gate[0], w_up[0], w_down[0]

    slot_of = slots_of(routes[:, 0], experts, capacity)
    selector = (slot_of[None, :] == jnp.arange(slots, dtype=jnp.int32)[:, None]).astype(BF)
    sent_cots = dot(selector, cotangent).astype(BF).reshape(experts, capacity, width)
    sent_cots, raw_tiles = lax.optimization_barrier((sent_cots, raw_tiles))
    own_cots = lax.all_to_all(sent_cots, DE, split_axis=0, concat_axis=0, tiled=True).reshape(slots, width)
    before, after = shifted(own_cots, 1), shifted(own_cots, -1)
    windows = window_rows(halo_rows(raw_tiles), tokens)
    windows = jnp.pad(windows, ((0, 0), (0, -PIX % 128)))
    windows = dot(selector, windows).astype(BF).reshape(experts, capacity, -1)
    windows, _ = lax.optimization_barrier((windows, own_cots))
    own_cells = lax.all_to_all(windows, DE, split_axis=0, concat_axis=0, tiled=True).reshape(slots, -1)
    middle = slots // 2
    upper, lower = before[:middle], after[middle:]
    opposite = [shifted(upper, 1), shifted(lower, -1)]
    own_cells, upper, lower = lax.optimization_barrier((own_cells, upper, lower))
    cots = [own_cots, before, after, *opposite]
    cells = [own_cells, shifted(own_cells, 1), shifted(own_cells, -1), shifted(own_cells, 2)]
    member = lax.axis_index("tp")
    sources = jnp.remainder(member + jnp.array([0, -1, 1, 2], jnp.int32), members)

    conv = jnp.pad(stem_matrix(stem_weight), ((0, -PIX % 128), (0, 0)))
    expert = lax.axis_index(DE)
    router_row = lax.dynamic_slice_in_dim(router_weight, expert, 1, axis=1).reshape(1, width)
    router_row = router_row.astype(F32)
    gain = norm_gain.reshape(1, width)
    core = lax.axis_index("core").reshape(1)
    place_at = jnp.concatenate([expert.reshape(1), core, sources])
    weights = (conv, embed_weight, w_gate, w_up, w_down)
    saved = layer(0, members, place_at, gain, router_row, cells[:1], cots[:1], weights, ())
    out_part, hidden, hidden_act, gate_cot, up_cot, out_cot, own, other = layer(
        1, members, place_at, gain, router_row, cells, cots[1:], weights, saved
    )
    out_share = lax.psum_scatter(out_part, "tp", scatter_dimension=0, tiled=True)
    mixed = out_share.reshape(experts, capacity, width)
    returned = lax.all_to_all(mixed, DE, split_axis=0, concat_axis=0, tiled=True)
    expert_mix = dot(selector, returned.reshape(slots, width), ((0,), (0,))).astype(BF)

    def weight_grads(ready):
        rows, gates, ups, acts, outs, _ = lax.optimization_barrier(
            (hidden, gate_cot, up_cot, hidden_act, out_cot, ready)
        )
        return (
            dot(rows, gates, ((0,), (0,))),
            dot(rows, ups, ((0,), (0,))),
            dot(acts, outs, ((0,), (0,))),
        )

    mine, theirs, grads = total_over_all(own, other, weight_grads)
    embed_total, router_total, gain_total, stem_total = finish(
        core, mine, theirs, embed_weight.shape[0], width, experts
    )
    stem_total = stem_total[:36, : stem_weight.shape[0]].reshape(3, 3, 4, -1).transpose(3, 2, 0, 1)
    return (
        expert_mix,
        grads[0][None],
        grads[1][None],
        grads[2][None],
        router_total.T,
        gain_total.reshape(width),
        embed_total,
        stem_total,
    )


def solution(mesh):
    owners, members = mesh.devices.shape
    fine = jax.sharding.Mesh(mesh.devices.reshape(owners // 2, 2, members), ("xz", "core", "tp"))
    return jax.shard_map(
        local,
        mesh=fine,
        in_specs=(
            P(None, DE_TP, None),
            P(),
            P(),
            P(),
            P(),
            P(DE, None, "tp"),
            P(DE, None, "tp"),
            P(DE, "tp", None),
            P(DE_TP, None),
            P(DE_TP, None),
        ),
        out_specs=(
            P(DE_TP, None),
            P(DE, None, "tp"),
            P(DE, None, "tp"),
            P(DE, "tp", None),
            P(),
            P(),
            P(),
            P(),
        ),
        check_vma=False,
    )
```
